256 devices in a mesh: section: 4 (over x), ctx: 16 (over z, core), tp: 4 (over y).
Axes of the slice: x: 4, y: 4, z: 8, core: 2. Of those that a mesh axis runs over, the one named last changes fastest.
Arguments:
- hidden_in: bfloat16 [4, 4096, 8192], P('section', 'ctx', 'tp'), may hold values from -6 to 6
- gate_in: bfloat16 [4, 2, 4096, 8192], P('section', None, 'ctx', 'tp'), may hold values from -8 to 8
- state_proj: bfloat16 [4, 2, 2, 4096, 512], P('section', None, None, 'ctx', 'tp'), may hold values from -6 to 6
- step_size: float32 [4, 2, 128, 4096], P('section', None, 'tp', 'ctx'), may hold values from 0.01 to 0.1
- log_decay: float32 [4, 2, 128, 4096], P('section', None, 'tp', 'ctx'), may hold values from -1 to 0
- request_ids: int32 [4, 4096], P('section', 'ctx'), may hold values from 0 to 3, never falling along the last dimension, each value on 1 to 2048 neighbouring positions
- conv_inner: float32 [4, 2, 4, 8192], P('section', None, None, 'tp'), may hold values from -3 to 3
- conv_state: float32 [4, 2, 4, 2, 512], P('section', None, None, None, 'tp'), may hold values from -3 to 3
- skip_gain: float32 [4, 2, 128], P('section', None, 'tp'), may hold values from 0.5 to 2
- norm_gain: float32 [4, 2, 8192], P('section', None, 'tp'), may hold values from 0.5 to 1.5
Outputs:
- hidden_out: bfloat16 [4, 4096, 8192], P('section', 'ctx', 'tp')
The draws below stay inside these ranges and needn't reach their ends.
Inputs may be any that keep to these rules, and one draw needn't show every extreme that they name: `request_ids`: request numbers never fall along the tokens of a section; each request covers 1 to 2048 tokens, and one covers exactly 2048.
All inputs are finite; a program needn't handle non-finite values.
Results may differ from the reference program's by a relative error of at most 0.007.
Values may be sent and summed in bfloat16 or wider, within the bound.
A program may use at most 128 MiB of HBM per device.

```python
import math
import jax
import jax.numpy as jnp
import numpy as np
from jax import lax

HEADS = 128
HDIM = 64
STATE = 128
GROUPS = 4
KCONV = 4
BLK = 128
MIXER_LAYERS = 2
INNER = 8192
SECTION_TOKENS = 4096
RELAY_SECTIONS = 4
REQS = 4
REQ_MOST = 2048


def draw_gate_in(key, part):
    shape_all = (RELAY_SECTIONS, MIXER_LAYERS, SECTION_TOKENS, HEADS * HDIM)
    lift = -1.0 + 2.5 * jnp.arange(HEADS * HDIM, dtype=jnp.float32) / (HEADS * HDIM)
    noise = jnp.clip(jax.random.normal(key, shape_all, jnp.float32), -6.0, 6.0)
    return (noise + lift).astype(jnp.bfloat16)


def draw_log_decay(key, part):
    every_key = jax.random.split(key, 6)
    head_shape = (RELAY_SECTIONS, MIXER_LAYERS, HEADS, 1)
    full_shape = (RELAY_SECTIONS, MIXER_LAYERS, HEADS, SECTION_TOKENS)
    surge_count = 4
    slow_share = 0.5
    slow_heads = jax.random.uniform(every_key[0], head_shape, jnp.float32) < slow_share
    slow_rate = jnp.exp(jax.random.uniform(every_key[1], head_shape, jnp.float32, jnp.log(0.1), jnp.log(1.5))) / REQ_MOST
    fast_rate = jnp.exp(jax.random.uniform(every_key[2], head_shape, jnp.float32, jnp.log(1.0 / 50.0), jnp.log(1.0 / 30.0)))
    baseline_rate = jnp.where(slow_heads, slow_rate, fast_rate)
    coarse_value = jnp.exp(jax.random.uniform(every_key[3], full_shape, jnp.float32, jnp.log(0.5), jnp.log(2.0)))
    token_places = jax.random.randint(every_key[4], (RELAY_SECTIONS, MIXER_LAYERS, 1, surge_count), 0, SECTION_TOKENS)
    surge_lengths = jnp.any(jnp.arange(SECTION_TOKENS)[:, None] == token_places[:, :, :, None, :], axis=-1)
    layer_depth = jax.random.uniform(every_key[5], full_shape, jnp.float32, 0.22, 0.69)
    return -(baseline_rate * coarse_value) - jnp.where(surge_lengths, layer_depth, 0.0)


def block_scale(stream_key, shape, cuts, least, top_value):
    level = 1.0
    for dim, parts in cuts:
        steps = jax.random.uniform(jax.random.fold_in(jax.random.fold_in(stream_key, 6), dim), (parts,), jnp.float32, least / len(cuts), top_value / len(cuts))
        level = level * jnp.repeat(jnp.exp(steps), shape[dim] // parts).reshape((-1,) + (1,) * (len(shape) - 1 - dim))
    return level


def split_up(count, total, most, skew):
    loads = [(1 << 20) // math.isqrt(grade ** skew) + 1 for grade in range(2, count + 1)]
    surplus, given = total - most - (count - 1), [1] * (count - 1)
    while surplus > 0:
        movable = [i for i in range(count - 1) if given[i] < most]
        whole, remaining = sum([loads[i] for i in movable]), surplus
        for i in movable:
            more = min(most - given[i], max(1, remaining * loads[i] // whole), surplus)
            given[i] = given[i] + more
            surplus = surplus - more
    return np.array([most] + given)


def ragged_sizes(rng, amount, total, bound, lean):
    if amount == 2:
        one = jax.random.randint(rng, (), max(1, total - bound), min(bound, total - 1) + 1)
        return jnp.stack([one, total - one])
    lengths = jnp.asarray(split_up(amount, total, bound, lean), jnp.int32)
    twos = (amount - 1) // 2
    donor, sink = lengths[1:1 + 2 * twos:2], lengths[2:2 + 2 * twos:2]
    room = jnp.minimum(donor - 1, bound - sink)
    moved = jax.random.randint(jax.random.fold_in(rng, 1), (twos,), 0, 1 << 20) % (room + 1)
    lengths = lengths.at[1:1 + 2 * twos:2].set(donor - moved).at[2:2 + 2 * twos:2].set(sink + moved)
    return lengths[jax.random.permutation(jax.random.fold_in(rng, 2), amount)]


def normal_values(rng, dims, deviation, most, shards=(), kind=jnp.bfloat16):
    entries = deviation * jax.random.normal(rng, dims, jnp.float32)
    if shards:
        entries = entries * block_scale(rng, dims, shards, -0.22, 0.18)
    return jnp.clip(entries, -most, most).astype(kind)


def setup_inputs(seed: int = 0) -> dict:
    key_of = jax.random.split(jax.random.key(seed), 11)
    hidden_in = normal_values(key_of[0], (RELAY_SECTIONS, SECTION_TOKENS, INNER), 1.0, 6.0, ((0, 4), (1, 16), (2, 4)))
    gate_in = draw_gate_in(jax.random.fold_in(key_of[10], 71), 0)
    state_proj = normal_values(key_of[2], (RELAY_SECTIONS, MIXER_LAYERS, 2, SECTION_TOKENS, GROUPS * STATE), 1.0, 6.0, ((0, 4), (3, 16), (4, 4)))
    step_size = jnp.clip(jnp.exp(math.log(0.1) - 2.3025851 * jax.random.uniform(key_of[3], (RELAY_SECTIONS, MIXER_LAYERS, HEADS, SECTION_TOKENS), jnp.float32) ** block_scale(key_of[3], (RELAY_SECTIONS, MIXER_LAYERS, HEADS, SECTION_TOKENS), ((0, 4), (2, 4), (3, 16)), -0.2, 0.2)), 0.01, 0.1)
    log_decay = draw_log_decay(jax.random.fold_in(key_of[10], 71), 0)
    request_ids = jax.vmap(lambda own: jnp.searchsorted(jnp.cumsum(ragged_sizes(own, REQS, SECTION_TOKENS, REQ_MOST, 1)), jnp.arange(SECTION_TOKENS), side="right"))(jax.random.split(key_of[5], RELAY_SECTIONS)).reshape((RELAY_SECTIONS, SECTION_TOKENS)).astype(jnp.int32)
    conv_inner = normal_values(key_of[6], (RELAY_SECTIONS, MIXER_LAYERS, KCONV, INNER), KCONV ** -0.5, 3.0, ((0, 4), (3, 4)), jnp.float32)
    conv_state = normal_values(key_of[7], (RELAY_SECTIONS, MIXER_LAYERS, KCONV, 2, GROUPS * STATE), KCONV ** -0.5, 3.0, ((0, 4), (4, 4)), jnp.float32)
    skip_gain = jnp.clip(jnp.exp(math.log(2.0) - 1.3862944 * jax.random.uniform(key_of[8], (RELAY_SECTIONS, MIXER_LAYERS, HEADS), jnp.float32) ** block_scale(key_of[8], (RELAY_SECTIONS, MIXER_LAYERS, HEADS), ((0, 4), (2, 4)), -0.2, 0.2)), 0.5, 2.0)
    norm_gain = jnp.clip(1.0 + 0.1 * jax.random.normal(key_of[9], (RELAY_SECTIONS, MIXER_LAYERS, INNER), jnp.float32), 0.5, 1.5)
    return {"hidden_in": hidden_in, "gate_in": gate_in, "state_proj": state_proj, "step_size": step_size, "log_decay": log_decay, "request_ids": request_ids, "conv_inner": conv_inner, "conv_state": conv_state, "skip_gain": skip_gain, "norm_gain": norm_gain}


def causal_conv(extended, ext_markers, markers, weights, count):
    summed = jnp.zeros(extended.shape[:-2] + (count, extended.shape[-1]), jnp.float32)
    for tap_idx in range(weights.shape[0]):
        window = lax.slice_in_dim(extended, tap_idx, tap_idx + count, axis=extended.ndim - 2)
        same_req = (ext_markers[tap_idx:tap_idx + count] == markers)[:, None]
        summed = summed + jnp.where(same_req, weights[tap_idx] * window, 0.0)
    return jax.nn.silu(summed).astype(jnp.bfloat16)

def mixer_whole(stream, gate_rows, proj_rows, step_rows, decay_rows, conv_w, conv_s, skip_w, gain_w, markers):
    tok_rows = stream.shape[0]
    head_group = HEADS // GROUPS
    block_count = tok_rows // BLK
    pad_rows = jnp.zeros((KCONV - 1, stream.shape[1]), jnp.float32)
    pad_proj = jnp.zeros((2, KCONV - 1, proj_rows.shape[2]), jnp.float32)
    pad_marks = jnp.zeros((KCONV - 1,), jnp.float32)
    ext_markers = jnp.concatenate([pad_marks, markers])
    xs_rows = causal_conv(jnp.concatenate([pad_rows, stream.astype(jnp.float32)], 0), ext_markers, markers, conv_w, tok_rows)
    bc_rows = causal_conv(jnp.concatenate([pad_proj, proj_rows.astype(jnp.float32)], 1), ext_markers, markers, conv_s[:, :, None, :], tok_rows)
    dx_rows = (step_rows.T[:, :, None] * xs_rows.reshape(tok_rows, HEADS, HDIM).astype(jnp.float32)).astype(jnp.bfloat16)
    cum_decay = jnp.cumsum(decay_rows.reshape(HEADS, block_count, BLK), axis=-1).transpose(1, 0, 2)
    b_blocks = bc_rows[0].reshape(block_count, BLK, GROUPS, STATE)
    c_blocks = bc_rows[1].reshape(block_count, BLK, GROUPS, STATE)
    dx_blocks = dx_rows.reshape(block_count, BLK, GROUPS, head_group, HDIM)
    mark_blocks = markers.reshape(block_count, BLK)
    lower = jnp.arange(BLK)[:, None] >= jnp.arange(BLK)[None, :]

    def one_block(carried, block_item):
        state_now, mark_now = carried
        c_blk, b_blk, dx_blk, cum_blk, mark_blk = block_item
        c_wide = c_blk.astype(jnp.float32)
        b_wide = b_blk.astype(jnp.float32)
        dx_wide = dx_blk.astype(jnp.float32)
        scores = jnp.einsum('tgn,sgn->gts', c_wide, b_wide)
        allowed = lower & (mark_blk[:, None] == mark_blk[None, :])
        gap_log = cum_blk[:, :, None] - cum_blk[:, None, :]
        decay_mat = jnp.where(allowed, jnp.exp(jnp.where(allowed, gap_log, 0.0)), 0.0)
        mix_weight = (scores[:, None] * decay_mat.reshape(GROUPS, head_group, BLK, BLK)).astype(jnp.bfloat16)
        y_intra = jnp.einsum('ghts,sghp->tghp', mix_weight.astype(jnp.float32), dx_wide)
        factor = jnp.where((mark_blk == mark_now)[None, :], jnp.exp(cum_blk), 0.0)
        y_state = jnp.einsum('tgn,ghnp->tghp', c_wide, state_now.reshape(GROUPS, head_group, STATE, HDIM), precision=lax.Precision.HIGHEST)
        y_state = y_state * factor.reshape(GROUPS, head_group, BLK).transpose(2, 0, 1)[..., None]
        last_cum = cum_blk[:, -1]
        last_mark = mark_blk[-1]
        tail_weight = jnp.where((mark_blk == last_mark)[None, :], jnp.exp(last_cum[:, None] - cum_blk), 0.0)
        b_weighted = (tail_weight.reshape(GROUPS, head_group, BLK).transpose(2, 0, 1)[..., None] * b_wide[:, :, None, :]).astype(jnp.bfloat16)
        block_sum = jnp.einsum('sghn,sghp->ghnp', b_weighted.astype(jnp.float32), dx_wide).reshape(HEADS, STATE, HDIM)
        new_state = jnp.where(last_mark == mark_now, jnp.exp(last_cum)[:, None, None] * state_now, 0.0) + block_sum
        return ((new_state, jnp.reshape(last_mark, (1,))), y_intra + y_state)
    start = (jnp.zeros((HEADS, STATE, HDIM), jnp.float32), jnp.zeros((1,), jnp.float32))
    _, y_blocks = lax.scan(one_block, start, (c_blocks, b_blocks, dx_blocks, cum_decay, mark_blocks))
    y_rows = y_blocks.reshape(tok_rows, HEADS * HDIM) + jnp.repeat(skip_w, HDIM)[None, :] * xs_rows.astype(jnp.float32)
    gated = y_rows * jax.nn.silu(gate_rows.astype(jnp.float32))
    mean_sq = lax.optimization_barrier(jnp.sum(gated * gated, axis=1)) / (HEADS * HDIM)
    return (stream.astype(jnp.float32) + gated * gain_w[None, :] * lax.rsqrt(mean_sq + 1e-05)[:, None]).astype(jnp.bfloat16)

def reference(hidden_in, gate_in, state_proj, step_size, log_decay, request_ids, conv_inner, conv_state, skip_gain, norm_gain):
    results = []
    for section_idx in range(RELAY_SECTIONS):
        markers = (request_ids[section_idx] + 1).astype(jnp.float32)
        stream = hidden_in[section_idx]
        for layer_idx in range(MIXER_LAYERS):
            stream = mixer_whole(stream, gate_in[section_idx, layer_idx], state_proj[section_idx, layer_idx], step_size[section_idx, layer_idx], log_decay[section_idx, layer_idx], conv_inner[section_idx, layer_idx], conv_state[section_idx, layer_idx], skip_gain[section_idx, layer_idx], norm_gain[section_idx, layer_idx], markers)
        results.append(stream)
    return jnp.roll(jnp.stack(results, 0), 1, axis=0)
```

```python
import functools

import jax
import jax.numpy as jnp
from jax import lax
from jax.experimental import pallas as pl
from jax.experimental.pallas import tpu as pltpu
from jax.sharding import PartitionSpec as P

HDIM = 64
BLK = 128
TOK = 256
CH = 2048
TILE = 256
NT = CH // TILE
HALF = NT // 2
LAYERS = 2
F32 = jnp.float32
BF16 = jnp.bfloat16
MESH = pl.DeviceIdType.MESH


def mm(a, b):
    return jnp.dot(a, b, preferred_element_type=F32)


def mm_nt(a, b):
    return lax.dot_general(a, b, (((1,), (1,)), ((), ())), preferred_element_type=F32)


def iota(shape, dim):
    return lax.broadcasted_iota(jnp.int32, shape, dim)


def parts(v, count):
    out = []
    for _ in range(count - 1):
        p = v.astype(BF16).astype(F32)
        out.append(p)
        v = v - p
    out.append(v)
    return out


def silu_of_half(h):
    return h + h * jnp.tanh(h)


def kernel(
    n_sec,
    n_ctx,
    n_tp,
    hid,
    gate,
    proj,
    step,
    decay,
    ids,
    cw,
    sw,
    skip,
    gain,
    out,
    uext,
    pext,
    idp,
    gbuf,
    mshift,
    e2a,
    e2b,
    e128,
    cts,
    va,
    vb,
    cum_s,
    cmat_s,
    bt_s,
    sc_s,
    xs_s,
    dx_s,
    bs0_s,
    l_s,
    l_r,
    sin_s,
    sout_s,
    x_s,
    xo_s,
    g1,
    g2,
    sq,
    ps_s,
    ps_r,
    r_s,
    in_sem,
    halo_sem,
    first_sem,
    l_sem,
    s_sem,
    x_sem,
    p_sem,
    o_sem,
):
    sec = lax.axis_index("section")
    c = lax.axis_index("ctx")
    tp = lax.axis_index("tp")
    z = lax.div(c, 2)
    k = lax.rem(c, 2)
    last_z = n_ctx // 2 - 1
    partner = c + 1 - 2 * k
    core0 = k == 0

    in_hid = pltpu.make_async_copy(hid.at[0], uext.at[0, pl.ds(BLK, TOK)], in_sem.at[0])
    in_hid.start()
    in_proj = []
    for l in range(LAYERS):
        for w in range(2):
            cp = pltpu.make_async_copy(
                proj.at[0, l, w],
                pext.at[l, pl.ds(BLK, TOK), pl.ds(w * 128, 128)],
                in_sem.at[1 + 2 * l + w],
            )
            cp.start()
            in_proj.append(cp)
    in_gate = [
        pltpu.make_async_copy(gate.at[0, l], gbuf.at[l], in_sem.at[5 + l]) for l in range(LAYERS)
    ]

    @pl.when(c == 0)
    def _():
        for l in range(LAYERS):
            uext[l, pl.ds(112, 16), :] = jnp.zeros((16, CH), BF16)
            pext[l, pl.ds(112, 16), :] = jnp.zeros((16, 256), BF16)
        idp[...] = jnp.full((1, TOK), -1, jnp.int32)

    @pl.when(z == 0)
    def _():
        sin_s[...] = jnp.zeros(sin_s.shape, BF16)

    bar = pltpu.get_barrier_semaphore()

    def greet(**where):
        pl.semaphore_signal(bar, inc=1, device_id=where, device_id_type=MESH)

    @pl.when(c >= 1)
    def _():
        greet(ctx=c - 1)

    @pl.when(c >= 2)
    def _():
        greet(ctx=c - 2)

    @pl.when(core0)
    def _():
        greet(ctx=c + 1)

    for d in range(1, n_tp):
        greet(tp=lax.rem(tp + d, n_tp))
    greet(section=lax.rem(sec + n_sec - 1, n_sec))

    q = iota((128, CH), 0)
    head = iota((128, CH), 1) // HDIM
    e2a[...] = jnp.where((q < 64) & (q % 32 == head), 1.0, 0.0).astype(BF16)
    e2b[...] = jnp.where((q >= 64) & (q % 32 == head), 1.0, 0.0).astype(BF16)
    q = iota((128, 4096), 0)
    head = iota((128, 4096), 1) // 128
    e128[...] = jnp.where((q < 96) & (q % 32 == head), 1.0, 0.0).astype(BF16)
    for l in range(LAYERS):
        uext[l, pl.ds(0, 112), :] = jnp.zeros((112, CH), BF16)
        pext[l, pl.ds(0, 112), :] = jnp.zeros((112, 256), BF16)

    in_hid.wait()
    for cp in in_proj:
        cp.wait()
    for cp in in_gate:
        cp.start()

    greeted = (
        jnp.where(c + 1 < n_ctx, 1, 0) + jnp.where(c + 2 < n_ctx, 1, 0) + k + (n_tp - 1) + 1
    )
    pl.semaphore_wait(bar, greeted)

    def halo_copy(l):
        return pltpu.make_async_remote_copy(
            src_ref=uext.at[l, pl.ds(BLK + TOK - 16, 16)],
            dst_ref=uext.at[l, pl.ds(112, 16)],
            send_sem=halo_sem.at[0, l],
            recv_sem=halo_sem.at[1, l],
            device_id={"ctx": c + 1},
            device_id_type=MESH,
        )

    def first_copies():
        return [
            pltpu.make_async_remote_copy(
                src_ref=ids,
                dst_ref=idp,
                send_sem=first_sem.at[0, 0],
                recv_sem=first_sem.at[1, 0],
                device_id={"ctx": c + 1},
                device_id_type=MESH,
            ),
            pltpu.make_async_remote_copy(
                src_ref=pext.at[:, pl.ds(BLK + TOK - 16, 16)],
                dst_ref=pext.at[:, pl.ds(112, 16)],
                send_sem=first_sem.at[0, 1],
                recv_sem=first_sem.at[1, 1],
                device_id={"ctx": c + 1},
                device_id_type=MESH,
            ),
        ]

    @pl.when(c + 1 < n_ctx)
    def _():
        for cp in first_copies():
            cp.start()
        halo_copy(0).start()

    @pl.when(c >= 1)
    def _():
        for cp in first_copies():
            cp.wait_recv()

    m_row = ids[...].astype(F32)
    m_old = idp[...].astype(F32)
    m_ext = jnp.concatenate([m_old[:, 128:], m_row], axis=1)
    m_prev = m_old[:, 255:256]
    m_e0 = m_row[:, 127:128]
    m_e1 = m_row[:, 255:256]
    m_col = jnp.broadcast_to(m_row, (128, TOK)).T
    for b in range(2):
        mine = m_col[b * BLK : (b + 1) * BLK]
        mine = jnp.concatenate([mine, mine], axis=1)
        same = mine == m_ext[:, b * BLK : b * BLK + 256]
        gap = iota((BLK, 256), 0) + BLK - iota((BLK, 256), 1)
        for j in range(3):
            mshift[b, pl.ds(j * BLK, BLK), :] = jnp.where(same & (gap == j + 1), 1.0, 0.0).astype(
                BF16
            )

    lane = iota((32, TOK), 1)

    def prep(l):
        for b in range(2):
            rows = pl.ds(b * BLK, BLK)
            moved = mm(mshift[b], pext[l, pl.ds(b * BLK, 256), :])
            now = pext[l, pl.ds((b + 1) * BLK, BLK), :].astype(F32)
            taps = [
                0.5 * jnp.concatenate([sw[0, l, t, 0:1, :], sw[0, l, t, 1:2, :]], axis=1)
                for t in range(4)
            ]
            h = taps[3] * now
            for j in range(3):
                h = h + taps[2 - j] * moved[j * BLK : (j + 1) * BLK]
            v = silu_of_half(h)
            bm = v[:, :128]
            cm = v[:, 128:].astype(BF16)
            cmat_s[l, rows, :] = cm
            bt_s[l, :, rows] = bm.T.astype(BF16)
            scores = mm_nt(cm, bm.astype(BF16))
            ok = (iota((BLK, BLK), 0) >= iota((BLK, BLK), 1)) & (
                m_col[b * BLK : (b + 1) * BLK] == m_row[:, b * BLK : (b + 1) * BLK]
            )
            sc_s[l, b] = jnp.where(ok, scores, 0.0)
        d3 = jnp.concatenate(parts(decay[0, l], 3), axis=0).astype(BF16)
        tri = jnp.where(iota((TOK, TOK), 0) <= iota((TOK, TOK), 1), 1.0, 0.0).astype(BF16)
        c3 = mm(d3, tri)
        cum = c3[0:32] + c3[32:64] + c3[64:96]
        for j in range(NT):
            cum_s[l, j, 0:4, :] = cum[4 * j : 4 * j + 4]
        zero = jnp.zeros((32, TOK), F32)
        cts[l] = jnp.concatenate(parts(cum, 3) + [zero], axis=0).T.astype(BF16)
        tot0 = cum[:, 127:128]
        tot1 = cum[:, 255:256]
        first = lane < BLK
        m_e = jnp.where(first[0:1], m_e0, m_e1)
        tail = jnp.where(first, tot0, tot1) - cum
        dt = step[0, l]
        w = dt * jnp.where(m_row == m_e, jnp.exp(jnp.minimum(tail, 0.0)), 0.0)
        va[l] = jnp.concatenate(parts(dt, 2) + parts(w, 2), axis=0).T.astype(BF16)
        f = jnp.where(m_row == m_prev, jnp.exp(jnp.minimum(cum, 0.0)), 0.0)
        f1 = jnp.where(
            (m_row == m_e0) & jnp.logical_not(first), jnp.exp(jnp.minimum(cum - tot0, 0.0)), 0.0
        )
        vb[l] = jnp.concatenate(parts(f, 2) + parts(f1, 2), axis=0).T.astype(BF16)

    prep(0)

    def l_copy(l, i):
        return pltpu.make_async_remote_copy(
            src_ref=l_s.at[l, HALF * (1 - k) + i],
            dst_ref=l_r.at[l, i],
            send_sem=l_sem.at[0, l, i],
            recv_sem=l_sem.at[1, l, i],
            device_id={"ctx": partner},
            device_id_type=MESH,
        )

    def s_copy(l, i):
        return pltpu.make_async_remote_copy(
            src_ref=sout_s.at[l, i],
            dst_ref=sin_s.at[l, i],
            send_sem=s_sem.at[0, l, i],
            recv_sem=s_sem.at[1, l, i],
            device_id={"ctx": c + 2},
            device_id_type=MESH,
        )

    def x_copy(l, i):
        return pltpu.make_async_remote_copy(
            src_ref=xo_s.at[l, i],
            dst_ref=x_s.at[l, HALF * k + i],
            send_sem=x_sem.at[0, l, i],
            recv_sem=x_sem.at[1, l, i],
            device_id={"ctx": partner},
            device_id_type=MESH,
        )

    def x_arrival(l, i):
        return pltpu.make_async_remote_copy(
            src_ref=xo_s.at[l, i],
            dst_ref=x_s.at[l, HALF * (1 - k) + i],
            send_sem=x_sem.at[0, l, i],
            recv_sem=x_sem.at[1, l, i],
            device_id={"ctx": partner},
            device_id_type=MESH,
        )

    def p_copy(l, d):
        return pltpu.make_async_remote_copy(
            src_ref=ps_s.at[l],
            dst_ref=ps_r.at[l, d - 1],
            send_sem=p_sem.at[0, l, d - 1],
            recv_sem=p_sem.at[1, l, d - 1],
            device_id={"tp": lax.rem(tp + d, n_tp)},
            device_id_type=MESH,
        )

    def o_copy(i):
        row = TOK - 32 * (i + 1)
        return pltpu.make_async_remote_copy(
            src_ref=uext.at[LAYERS, pl.ds(pl.multiple_of(BLK + row, 32), 32)],
            dst_ref=out.at[0, pl.ds(pl.multiple_of(row, 32), 32)],
            send_sem=o_sem.at[0, i],
            recv_sem=o_sem.at[1, i],
            device_id={"section": lax.rem(sec + 1, n_sec)},
            device_id_type=MESH,
        )

    def local_part(l, i):
        tile = lax.rem(i + HALF * (1 - k), NT)
        cols = pl.ds(pl.multiple_of(tile * TILE, TILE), TILE)
        taps = [0.5 * cw[0, l, pl.ds(t, 1), cols] for t in range(4)]
        ea, eb = e2a[:, cols], e2b[:, cols]
        sums = []
        for b in range(2):
            rows = pl.ds(b * BLK, BLK)
            moved = mm(mshift[b], uext[l, pl.ds(b * BLK, 256), cols])
            h = taps[3] * uext[l, pl.ds((b + 1) * BLK, BLK), cols].astype(F32)
            for j in range(3):
                h = h + taps[2 - j] * moved[j * BLK : (j + 1) * BLK]
            xs = silu_of_half(h).astype(BF16)
            xs_s[rows, cols] = xs
            xs = xs.astype(F32)
            v = va[l, rows, :]
            dx_s[rows, cols] = (mm(v, ea) * xs).astype(BF16)
            sums.append(mm(bt_s[l, :, rows], (mm(v, eb) * xs).astype(BF16)))
        vend = vb[l, pl.ds(TOK - 16, 16), :]
        d_all = mm(vend, ea)[15:16]
        d_blk = mm(vend, eb)[15:16]
        bs0_s[tile] = sums[0].astype(BF16)
        l_s[l, tile, pl.ds(0, 128), :] = (d_blk * sums[0] + sums[1]).astype(BF16)
        hi, lo = parts(d_all, 2)
        row = iota((16, TILE), 0)
        l_s[l, tile, pl.ds(128, 16), :] = jnp.where(
            row == 0, hi, jnp.where(row == 1, lo, 0.0)
        ).astype(BF16)

    def chain(l, i):
        l_copy(l, i).wait_recv()

        @pl.when(z > 0)
        def _():
            s_copy(l, i).wait_recv()

        tile = HALF * k + i

        def both(ref):
            d = ref[pl.ds(128, 16), :].astype(F32)
            return ref[pl.ds(0, 128), :].astype(F32), d[0:1] + d[1:2]

        mine, d_mine = both(l_s.at[l, tile])
        other, d_other = both(l_r.at[l, i])
        s = sin_s[l, i].astype(F32)
        x1 = jnp.where(core0, mine, other) + jnp.where(core0, d_mine, d_other) * s
        end = jnp.where(core0, other, mine) + jnp.where(core0, d_other, d_mine) * x1
        sout_s[l, i] = end.astype(BF16)

        @pl.when(z < last_z)
        def _():
            s_copy(l, i).start()

        x_s[l, tile] = jnp.where(core0, s, x1).astype(BF16)
        xo_s[l, i] = jnp.where(core0, x1, s).astype(BF16)
        x_copy(l, i).start()

    low = iota((BLK, 128), 1) < HDIM
    low_row = iota((1, 128), 1) < HDIM

    def intra(l, tile):
        cols = pl.ds(pl.multiple_of(tile * TILE, TILE), TILE)
        for b in range(2):
            rows = pl.ds(b * BLK, BLK)
            scores = sc_s[l, b]
            ys = []
            for p in range(2):
                h0 = 4 * tile + 2 * p
                pair = pl.ds(pl.multiple_of(tile * TILE + p * 128, 128), 128)
                ct = mm(
                    cts[l, rows, :],
                    e128[:, pl.ds(pl.multiple_of(tile * 512 + p * 256, 256), 256)],
                )
                mix = []
                for o in range(2):
                    gap = ct[:, o * 128 : (o + 1) * 128] - cum_s[l, tile, 2 * p + o : 2 * p + o + 1, rows]
                    mix.append((scores * jnp.exp(jnp.minimum(gap, 0.0))).astype(BF16))
                dx = dx_s[rows, pair].astype(F32)
                both = jnp.concatenate(
                    [jnp.where(low, dx, 0.0), jnp.where(low, 0.0, dx)], axis=0
                ).astype(BF16)
                y = mm(jnp.concatenate(mix, axis=1), both)
                gains = jnp.where(low_row, skip[0, l, h0], skip[0, l, h0 + 1])
                ys.append(y + gains * xs_s[rows, pair].astype(F32))
            y = jnp.concatenate(ys, axis=1)
            v = vb[l, rows, :]
            if b == 1:
                y = y + mm(v, e2b[:, cols]) * mm(cmat_s[l, rows, :], bs0_s[tile])
            h = 0.5 * gbuf[l, rows, cols].astype(F32)
            sg = silu_of_half(h)
            g1[rows, cols] = y * sg
            g2[rows, cols] = mm(v, e2a[:, cols]) * sg

    def layer(l, carry):
        @pl.when(c >= 1)
        def _():
            halo_copy(l).wait_recv()

        def a_step(i, carry):
            local_part(l, i)

            @pl.when(i < HALF)
            def _():
                l_copy(l, i).start()

            return carry

        lax.fori_loop(0, NT, a_step, 0)

        early = (l == 1) | (z <= 1)

        @pl.when(l == 0)
        def _():
            for cp in in_gate:
                cp.wait()

        def b_step(i, carry):
            @pl.when(early)
            def _():
                chain(l, i)

            intra(l, 2 * i)
            intra(l, 2 * i + 1)
            return carry

        lax.fori_loop(0, HALF, b_step, 0)

        @pl.when(l == 0)
        def _():
            prep(1)

        def c_step(i, carry):
            @pl.when(jnp.logical_not(early))
            def _():
                chain(l, i)

            return carry

        lax.fori_loop(0, HALF, c_step, 0)

        sq[...] = jnp.zeros((TOK, 128), F32)

        def d_step(i, carry):
            @pl.when(i >= HALF)
            def _():
                x_arrival(l, i - HALF).wait_recv()

            tile = lax.rem(i + HALF * k, NT)
            cols = pl.ds(pl.multiple_of(tile * TILE, TILE), TILE)
            g = g1[:, cols] + g2[:, cols] * mm(cmat_s[l], x_s[l, tile])
            g1[:, cols] = g
            g = g * g
            sq[...] += g[:, :128] + g[:, 128:]
            return carry

        lax.fori_loop(0, NT, d_step, 0)

        hi, lo = parts(sq[...], 2)
        ones = jnp.ones((16, 128), BF16)
        total = (mm_nt(ones, hi.astype(BF16)) + mm_nt(ones, lo.astype(BF16)))[0:8]
        ps_s[l] = total
        for d in range(1, n_tp):
            p_copy(l, d).start()
        for d in range(1, n_tp):
            p_copy(l, d).wait_recv()
            total = total + ps_r[l, d - 1]
        scale = lax.rsqrt(total[0:1] / (CH * n_tp) + 1e-05)
        r_s[...] = jnp.broadcast_to(scale, (128, TOK)).T

        def e_step(i, carry):
            row = TOK - 32 * (i + 1)
            rows = pl.ds(pl.multiple_of(row, 32), 32)
            ext = pl.ds(pl.multiple_of(BLK + row, 32), 32)
            r = r_s[rows, :]
            for t in range(CH // 128):
                cols = pl.ds(t * 128, 128)
                gains = jnp.where(l == 0, gain[0, 0:1, cols], gain[0, 1:2, cols])
                uext[l + 1, ext, cols] = (
                    uext[l, ext, cols].astype(F32) + g1[rows, cols] * (gains * r)
                ).astype(BF16)

            @pl.when((l == 0) & (i == 0) & (c + 1 < n_ctx))
            def _():
                halo_copy(1).start()

            @pl.when(l == LAYERS - 1)
            def _():
                o_copy(i).start()

            return carry

        lax.fori_loop(0, TOK // 32, e_step, 0)
        return carry

    lax.fori_loop(0, LAYERS, layer, 0)

    @pl.when(c + 1 < n_ctx)
    def _():
        for cp in first_copies():
            cp.wait_send()
        for l in range(LAYERS):
            halo_copy(l).wait_send()

    def sent(n, carry):
        l, i = n // HALF, lax.rem(n, HALF)
        l_copy(l, i).wait_send()
        x_copy(l, i).wait_send()

        @pl.when(z < last_z)
        def _():
            s_copy(l, i).wait_send()

        return carry

    lax.fori_loop(0, LAYERS * HALF, sent, 0)
    for l in range(LAYERS):
        for d in range(1, n_tp):
            p_copy(l, d).wait_send()

    def moved(i, carry):
        o_copy(i).wait_send()
        o_copy(i).wait_recv()
        return carry

    lax.fori_loop(0, TOK // 32, moved, 0)


def per_device(sizes, *args):
    hbm = pl.BlockSpec(memory_space=pl.ANY)
    vmem = pl.BlockSpec(memory_space=pltpu.VMEM)
    smem = pl.BlockSpec(memory_space=pltpu.SMEM)
    dma = pltpu.SemaphoreType.DMA
    n_tp = sizes[2]
    return pl.pallas_call(
        functools.partial(kernel, *sizes),
        out_shape=jax.ShapeDtypeStruct((1, TOK, CH), BF16),
        in_specs=[hbm, hbm, hbm, vmem, vmem, vmem, vmem, vmem, smem, vmem],
        out_specs=hbm,
        scratch_shapes=[
            pltpu.VMEM((LAYERS + 1, BLK + TOK, CH), BF16),
            pltpu.VMEM((LAYERS, BLK + TOK, 256), BF16),
            pltpu.VMEM((1, TOK), jnp.int32),
            pltpu.VMEM((LAYERS, TOK, CH), BF16),
            pltpu.VMEM((2, 3 * BLK, 256), BF16),
            pltpu.VMEM((128, CH), BF16),
            pltpu.VMEM((128, CH), BF16),
            pltpu.VMEM((128, 4096), BF16),
            pltpu.VMEM((LAYERS, TOK, 128), BF16),
            pltpu.VMEM((LAYERS, TOK, 128), BF16),
            pltpu.VMEM((LAYERS, TOK, 128), BF16),
            pltpu.VMEM((LAYERS, NT, 8, TOK), F32),
            pltpu.VMEM((LAYERS, TOK, 128), BF16),
            pltpu.VMEM((LAYERS, 128, TOK), BF16),
            pltpu.VMEM((LAYERS, 2, BLK, BLK), F32),
            pltpu.VMEM((TOK, CH), BF16),
            pltpu.VMEM((TOK, CH), BF16),
            pltpu.VMEM((NT, 128, TILE), BF16),
            pltpu.VMEM((LAYERS, NT, 144, TILE), BF16),
            pltpu.VMEM((LAYERS, HALF, 144, TILE), BF16),
            pltpu.VMEM((LAYERS, HALF, 128, TILE), BF16),
            pltpu.VMEM((LAYERS, HALF, 128, TILE), BF16),
            pltpu.VMEM((LAYERS, NT, 128, TILE), BF16),
            pltpu.VMEM((LAYERS, HALF, 128, TILE), BF16),
            pltpu.VMEM((TOK, CH), F32),
            pltpu.VMEM((TOK, CH), F32),
            pltpu.VMEM((TOK, 128), F32),
            pltpu.VMEM((LAYERS, 8, TOK), F32),
            pltpu.VMEM((LAYERS, max(n_tp - 1, 1), 8, TOK), F32),
            pltpu.VMEM((TOK, 128), F32),
            dma((7,)),
            dma((2, LAYERS)),
            dma((2, 2)),
            dma((2, LAYERS, HALF)),
            dma((2, LAYERS, HALF)),
            dma((2, LAYERS, HALF)),
            dma((2, LAYERS, max(n_tp - 1, 1))),
            dma((2, TOK // 32)),
        ],
        compiler_params=pltpu.CompilerParams(
            collective_id=0, has_side_effects=True, vmem_limit_bytes=48 * 1024 * 1024
        ),
        cost_estimate=pl.CostEstimate(
            flops=2_000_000_000, bytes_accessed=6_000_000, transcendentals=6_000_000
        ),
        name="mixer",
    )(*args)


def solution(mesh):
    in_specs = (
        P("section", "ctx", "tp"),
        P("section", None, "ctx", "tp"),
        P("section", None, None, "ctx", "tp"),
        P("section", None, "tp", "ctx"),
        P("section", None, "tp", "ctx"),
        P("section", "ctx"),
        P("section", None, None, "tp"),
        P("section", None, None, None, "tp"),
        P("section", None, "tp"),
        P("section", None, "tp"),
    )
    out_specs = P("section", "ctx", "tp")
    sizes = tuple(mesh.shape[a] for a in ("section", "ctx", "tp"))
    return jax.shard_map(
        functools.partial(per_device, sizes),
        mesh=mesh,
        in_specs=in_specs,
        out_specs=out_specs,
        check_vma=False,
    )
```

```python
import functools

import jax
import jax.numpy as jnp
from jax import lax
from jax.experimental import pallas as pl
from jax.experimental.pallas import tpu as pltpu
from jax.sharding import PartitionSpec as P

HDIM = 64
BLK = 128
TOK = 256
CH = 2048
TILE = 256
NT = CH // TILE
HALF = NT // 2
HC = 2 * HALF
RC = TOK // 32
ROUND = RC // 4
LAG = 4
LAYERS = 2
F32 = jnp.float32
BF16 = jnp.bfloat16
MESH = pl.DeviceIdType.MESH


def mm(a, b):
    return jnp.dot(a, b, preferred_element_type=F32)


def mm_nt(a, b):
    return lax.dot_general(a, b, (((1,), (1,)), ((), ())), preferred_element_type=F32)


def iota(shape, dim):
    return lax.broadcasted_iota(jnp.int32, shape, dim)


def parts(v, count):
    out = []
    for _ in range(count - 1):
        p = v.astype(BF16).astype(F32)
        out.append(p)
        v = v - p
    out.append(v)
    return out


def silu_of_half(h):
    return h + h * jnp.tanh(h)


def kernel(
    n_sec,
    n_ctx,
    n_tp,
    hid,
    gate,
    proj,
    step_h,
    decay_h,
    ids_h,
    cw_h,
    sw_h,
    skip_h,
    gain_h,
    out,
    step,
    decay,
    ids,
    cw,
    sw,
    skip,
    gain,
    uext,
    pext,
    idp,
    gbuf,
    mshift,
    e2a,
    e2b,
    e128,
    cts,
    va,
    vb,
    cum_s,
    cmat_s,
    bt_s,
    sc_s,
    xs_s,
    dx_s,
    bs0_s,
    l_s,
    l_r,
    sin_s,
    sout_s,
    x_s,
    xo_s,
    g1,
    g2,
    sq,
    ps_s,
    ps_r,
    r_s,
    in_sem,
    halo_sem,
    first_sem,
    l_sem,
    s_sem,
    x_sem,
    p_sem,
    o_sem,
    r_sem,
    relay,
):
    sec = lax.axis_index("section")
    c = lax.axis_index("ctx")
    tp = lax.axis_index("tp")
    z = lax.div(c, 2)
    k = lax.rem(c, 2)
    last_z = n_ctx // 2 - 1
    partner = c + 1 - 2 * k
    core0 = k == 0

    in_small = []
    for n, (src, dst) in enumerate(
        [
            (ids_h, ids),
            (decay_h, decay),
            (step_h, step),
            (sw_h, sw),
            (cw_h, cw),
            (skip_h, skip),
            (gain_h, gain),
        ]
    ):
        cp = pltpu.make_async_copy(src, dst, in_sem.at[7 + n])
        cp.start()
        in_small.append(cp)
    in_hid = pltpu.make_async_copy(hid.at[0], uext.at[0, pl.ds(BLK, TOK)], in_sem.at[0])
    in_hid.start()
    in_proj = []
    for l in range(LAYERS):
        for w in range(2):
            cp = pltpu.make_async_copy(
                proj.at[0, l, w],
                pext.at[l, pl.ds(BLK, TOK), pl.ds(w * 128, 128)],
                in_sem.at[1 + 2 * l + w],
            )
            cp.start()
            in_proj.append(cp)
    in_gate = [
        pltpu.make_async_copy(gate.at[0, l], gbuf.at[l], in_sem.at[5 + l]) for l in range(LAYERS)
    ]

    @pl.when(c == 0)
    def _():
        for l in range(LAYERS):
            uext[l, pl.ds(112, 16), :] = jnp.zeros((16, CH), BF16)
            pext[l, pl.ds(112, 16), :] = jnp.zeros((16, 256), BF16)
        idp[...] = jnp.full((1, TOK), -1, jnp.int32)

    @pl.when(z == 0)
    def _():
        sin_s[...] = jnp.zeros(sin_s.shape, BF16)

    bar = pltpu.get_barrier_semaphore()

    def greet(**where):
        pl.semaphore_signal(bar, inc=1, device_id=where, device_id_type=MESH)

    @pl.when(c >= 1)
    def _():
        greet(ctx=c - 1)

    @pl.when(c >= 2)
    def _():
        greet(ctx=c - 2)

    @pl.when(core0)
    def _():
        greet(ctx=c + 1)

    for d in range(1, n_tp):
        greet(tp=lax.rem(tp + d, n_tp))
    greet(section=lax.rem(sec + n_sec - 1, n_sec))
    if n_sec > 2:
        greet(section=lax.rem(sec + 1, n_sec))

    q = iota((128, CH), 0)
    head = iota((128, CH), 1) // HDIM
    e2a[...] = jnp.where((q < 64) & (q % 32 == head), 1.0, 0.0).astype(BF16)
    e2b[...] = jnp.where((q >= 64) & (q % 32 == head), 1.0, 0.0).astype(BF16)
    q = iota((128, 4096), 0)
    head = iota((128, 4096), 1) // 128
    e128[...] = jnp.where((q < 96) & (q % 32 == head), 1.0, 0.0).astype(BF16)
    for l in range(LAYERS):
        uext[l, pl.ds(0, 112), :] = jnp.zeros((112, CH), BF16)
        pext[l, pl.ds(0, 112), :] = jnp.zeros((112, 256), BF16)

    in_hid.wait()
    for cp in in_proj + in_small:
        cp.wait()
    for cp in in_gate:
        cp.start()

    greeted = (
        jnp.where(c + 1 < n_ctx, 1, 0) + jnp.where(c + 2 < n_ctx, 1, 0) + k + (n_tp - 1) + min(n_sec - 1, 2)
    )
    pl.semaphore_wait(bar, greeted)

    def halo_copy(l):
        return pltpu.make_async_remote_copy(
            src_ref=uext.at[l, pl.ds(BLK + TOK - 16, 16)],
            dst_ref=uext.at[l, pl.ds(112, 16)],
            send_sem=halo_sem.at[0, l],
            recv_sem=halo_sem.at[1, l],
            device_id={"ctx": c + 1},
            device_id_type=MESH,
        )

    def first_copies():
        return [
            pltpu.make_async_remote_copy(
                src_ref=ids,
                dst_ref=idp,
                send_sem=first_sem.at[0, 0],
                recv_sem=first_sem.at[1, 0],
                device_id={"ctx": c + 1},
                device_id_type=MESH,
            ),
            pltpu.make_async_remote_copy(
                src_ref=pext.at[:, pl.ds(BLK + TOK - 16, 16)],
                dst_ref=pext.at[:, pl.ds(112, 16)],
                send_sem=first_sem.at[0, 1],
                recv_sem=first_sem.at[1, 1],
                device_id={"ctx": c + 1},
                device_id_type=MESH,
            ),
        ]

    @pl.when(c + 1 < n_ctx)
    def _():
        for cp in first_copies():
            cp.start()
        halo_copy(0).start()

    @pl.when(c >= 1)
    def _():
        for cp in first_copies():
            cp.wait_recv()

    m_row = ids[...].astype(F32)
    m_old = idp[...].astype(F32)
    m_ext = jnp.concatenate([m_old[:, 128:], m_row], axis=1)
    m_prev = m_old[:, 255:256]
    m_e0 = m_row[:, 127:128]
    m_e1 = m_row[:, 255:256]
    m_col = jnp.broadcast_to(m_row, (128, TOK)).T
    for b in range(2):
        mine = m_col[b * BLK : (b + 1) * BLK]
        mine = jnp.concatenate([mine, mine], axis=1)
        same = mine == m_ext[:, b * BLK : b * BLK + 256]
        gap = iota((BLK, 256), 0) + BLK - iota((BLK, 256), 1)
        for j in range(3):
            mshift[b, pl.ds(j * BLK, BLK), :] = jnp.where(same & (gap == j + 1), 1.0, 0.0).astype(
                BF16
            )

    lane = iota((32, TOK), 1)

    def prep(l):
        for b in range(2):
            rows = pl.ds(b * BLK, BLK)
            moved = mm(mshift[b], pext[l, pl.ds(b * BLK, 256), :])
            now = pext[l, pl.ds((b + 1) * BLK, BLK), :].astype(F32)
            taps = [
                0.5 * jnp.concatenate([sw[0, l, t, 0:1, :], sw[0, l, t, 1:2, :]], axis=1)
                for t in range(4)
            ]
            h = taps[3] * now
            for j in range(3):
                h = h + taps[2 - j] * moved[j * BLK : (j + 1) * BLK]
            v = silu_of_half(h)
            bm = v[:, :128]
            cm = v[:, 128:].astype(BF16)
            cmat_s[l, rows, :] = cm
            bt_s[l, :, rows] = bm.T.astype(BF16)
            scores = mm_nt(cm, bm.astype(BF16))
            ok = (iota((BLK, BLK), 0) >= iota((BLK, BLK), 1)) & (
                m_col[b * BLK : (b + 1) * BLK] == m_row[:, b * BLK : (b + 1) * BLK]
            )
            sc_s[l, b] = jnp.where(ok, scores, 0.0)
        d3 = jnp.concatenate(parts(decay[0, l], 3), axis=0).astype(BF16)
        tri = jnp.where(iota((TOK, TOK), 0) <= iota((TOK, TOK), 1), 1.0, 0.0).astype(BF16)
        c3 = mm(d3, tri)
        cum = c3[0:32] + c3[32:64] + c3[64:96]
        for j in range(NT):
            cum_s[l, j, 0:4, :] = cum[4 * j : 4 * j + 4]
        zero = jnp.zeros((32, TOK), F32)
        cts[l] = jnp.concatenate(parts(cum, 3) + [zero], axis=0).T.astype(BF16)
        tot0 = cum[:, 127:128]
        tot1 = cum[:, 255:256]
        first = lane < BLK
        m_e = jnp.where(first[0:1], m_e0, m_e1)
        tail = jnp.where(first, tot0, tot1) - cum
        dt = step[0, l]
        w = dt * jnp.where(m_row == m_e, jnp.exp(jnp.minimum(tail, 0.0)), 0.0)
        va[l] = jnp.concatenate(parts(dt, 2) + parts(w, 2), axis=0).T.astype(BF16)
        f = jnp.where(m_row == m_prev, jnp.exp(jnp.minimum(cum, 0.0)), 0.0)
        f1 = jnp.where(
            (m_row == m_e0) & jnp.logical_not(first), jnp.exp(jnp.minimum(cum - tot0, 0.0)), 0.0
        )
        vb[l] = jnp.concatenate(parts(f, 2) + parts(f1, 2), axis=0).T.astype(BF16)

    prep(0)

    def l_copy(l, i):
        return pltpu.make_async_remote_copy(
            src_ref=l_s.at[l, HALF * (1 - k) + i],
            dst_ref=l_r.at[l, i],
            send_sem=l_sem.at[0, l, i],
            recv_sem=l_sem.at[1, l, i],
            device_id={"ctx": partner},
            device_id_type=MESH,
        )

    def s_copy(l, i):
        return pltpu.make_async_remote_copy(
            src_ref=sout_s.at[l, i],
            dst_ref=sin_s.at[l, i],
            send_sem=s_sem.at[0, l, i],
            recv_sem=s_sem.at[1, l, i],
            device_id={"ctx": c + 2},
            device_id_type=MESH,
        )

    def half_tile(i):
        return pl.ds(pl.multiple_of(lax.rem(i, 2) * 128, 128), 128)

    def x_copy(l, i):
        return pltpu.make_async_remote_copy(
            src_ref=xo_s.at[l, i],
            dst_ref=x_s.at[l, HALF * k + lax.div(i, 2), :, half_tile(i)],
            send_sem=x_sem.at[0, l, i],
            recv_sem=x_sem.at[1, l, i],
            device_id={"ctx": partner},
            device_id_type=MESH,
        )

    def x_arrival(l, i):
        return pltpu.make_async_remote_copy(
            src_ref=xo_s.at[l, i],
            dst_ref=x_s.at[l, HALF * (1 - k) + lax.div(i, 2), :, half_tile(i)],
            send_sem=x_sem.at[0, l, i],
            recv_sem=x_sem.at[1, l, i],
            device_id={"ctx": partner},
            device_id_type=MESH,
        )

    def p_copy(l, d):
        return pltpu.make_async_remote_copy(
            src_ref=ps_s.at[l],
            dst_ref=ps_r.at[l, d - 1],
            send_sem=p_sem.at[0, l, d - 1],
            recv_sem=p_sem.at[1, l, d - 1],
            device_id={"tp": lax.rem(tp + d, n_tp)},
            device_id_type=MESH,
        )

    def o_copy(i):
        row = TOK - 32 * (i + 1)
        return pltpu.make_async_remote_copy(
            src_ref=uext.at[LAYERS, pl.ds(pl.multiple_of(BLK + row, 32), 32)],
            dst_ref=out.at[0, pl.ds(pl.multiple_of(row, 32), 32)],
            send_sem=o_sem.at[0, i],
            recv_sem=o_sem.at[1, i],
            device_id={"section": lax.rem(sec + 1, n_sec)},
            device_id_type=MESH,
        )

    def round_copy(i, hop):
        row = TOK - 32 * (i + 1)
        return pltpu.make_async_remote_copy(
            src_ref=uext.at[LAYERS, pl.ds(BLK + row, 32)] if hop == 0 else relay.at[hop - 1, i],
            dst_ref=out.at[0, pl.ds(row, 32)] if hop == n_sec - 2 else relay.at[hop, i],
            send_sem=r_sem.at[0, hop, i],
            recv_sem=r_sem.at[1, hop, i],
            device_id={"section": lax.rem(sec + n_sec - 1, n_sec)},
            device_id_type=MESH,
        )

    def local_part(l, i):
        tile = lax.rem(i + HALF * (1 - k), NT)
        cols = pl.ds(pl.multiple_of(tile * TILE, TILE), TILE)
        taps = [0.5 * cw[0, l, pl.ds(t, 1), cols] for t in range(4)]
        ea, eb = e2a[:, cols], e2b[:, cols]
        sums = []
        for b in range(2):
            rows = pl.ds(b * BLK, BLK)
            moved = mm(mshift[b], uext[l, pl.ds(b * BLK, 256), cols])
            h = taps[3] * uext[l, pl.ds((b + 1) * BLK, BLK), cols].astype(F32)
            for j in range(3):
                h = h + taps[2 - j] * moved[j * BLK : (j + 1) * BLK]
            xs = silu_of_half(h).astype(BF16)
            xs_s[rows, cols] = xs
            xs = xs.astype(F32)
            v = va[l, rows, :]
            dx_s[rows, cols] = (mm(v, ea) * xs).astype(BF16)
            sums.append(mm(bt_s[l, :, rows], (mm(v, eb) * xs).astype(BF16)))
        vend = vb[l, pl.ds(TOK - 16, 16), :]
        d_all = mm(vend, ea)[15:16]
        d_blk = mm(vend, eb)[15:16]
        bs0_s[tile] = sums[0].astype(BF16)
        l_s[l, tile, pl.ds(0, 128), :] = (d_blk * sums[0] + sums[1]).astype(BF16)
        hi, lo = parts(d_all, 2)
        row = iota((16, TILE), 0)
        l_s[l, tile, pl.ds(128, 16), :] = jnp.where(
            row == 0, hi, jnp.where(row == 1, lo, 0.0)
        ).astype(BF16)

    def chain(l, i):
        @pl.when(lax.rem(i, 2) == 0)
        def _():
            l_copy(l, lax.div(i, 2)).wait_recv()

        @pl.when(z > 0)
        def _():
            s_copy(l, i).wait_recv()

        tile = HALF * k + lax.div(i, 2)
        lanes = half_tile(i)

        def both(ref):
            d = ref[pl.ds(128, 16), lanes].astype(F32)
            return ref[pl.ds(0, 128), lanes].astype(F32), d[0:1] + d[1:2]

        mine, d_mine = both(l_s.at[l, tile])
        other, d_other = both(l_r.at[l, lax.div(i, 2)])
        s = sin_s[l, i].astype(F32)
        x1 = jnp.where(core0, mine, other) + jnp.where(core0, d_mine, d_other) * s
        end = jnp.where(core0, other, mine) + jnp.where(core0, d_other, d_mine) * x1
        sout_s[l, i] = end.astype(BF16)

        @pl.when(z < last_z)
        def _():
            s_copy(l, i).start()

        x_s[l, tile, :, lanes] = jnp.where(core0, s, x1).astype(BF16)
        xo_s[l, i] = jnp.where(core0, x1, s).astype(BF16)
        x_copy(l, i).start()

    low = iota((BLK, 128), 1) < HDIM
    low_row = iota((1, 128), 1) < HDIM

    def intra(l, tile):
        cols = pl.ds(pl.multiple_of(tile * TILE, TILE), TILE)
        for b in range(2):
            rows = pl.ds(b * BLK, BLK)
            scores = sc_s[l, b]
            ys = []
            for p in range(2):
                h0 = 4 * tile + 2 * p
                pair = pl.ds(pl.multiple_of(tile * TILE + p * 128, 128), 128)
                ct = mm(
                    cts[l, rows, :],
                    e128[:, pl.ds(pl.multiple_of(tile * 512 + p * 256, 256), 256)],
                )
                mix = []
                for o in range(2):
                    gap = ct[:, o * 128 : (o + 1) * 128] - cum_s[l, tile, 2 * p + o : 2 * p + o + 1, rows]
                    mix.append((scores * jnp.exp(jnp.minimum(gap, 0.0))).astype(BF16))
                dx = dx_s[rows, pair].astype(F32)
                both = jnp.concatenate(
                    [jnp.where(low, dx, 0.0), jnp.where(low, 0.0, dx)], axis=0
                ).astype(BF16)
                y = mm(jnp.concatenate(mix, axis=1), both)
                gains = jnp.where(low_row, skip[0, l, h0], skip[0, l, h0 + 1])
                ys.append(y + gains * xs_s[rows, pair].astype(F32))
            y = jnp.concatenate(ys, axis=1)
            v = vb[l, rows, :]
            if b == 1:
                y = y + mm(v, e2b[:, cols]) * mm(cmat_s[l, rows, :], bs0_s[tile])
            h = 0.5 * gbuf[l, rows, cols].astype(F32)
            sg = silu_of_half(h)
            g1[rows, cols] = y * sg
            g2[rows, cols] = mm(v, e2a[:, cols]) * sg

    def layer(l, carry):
        @pl.when(c >= 1)
        def _():
            halo_copy(l).wait_recv()

        def a_step(i, carry):
            local_part(l, i)

            @pl.when(i < HALF)
            def _():
                l_copy(l, i).start()

            return carry

        lax.fori_loop(0, NT, a_step, 0)

        @pl.when(l == 0)
        def _():
            for cp in in_gate:
                cp.wait()

        lag = jnp.where(l == 0, jnp.minimum(LAG * z, NT), 0)
        prep_at = jnp.where(z <= 2, 2 * NT - 1, NT)

        def b_step(i, carry):
            @pl.when((l == 0) & (i == prep_at))
            def _():
                prep(1)

            @pl.when((i >= lag) & (i < lag + HC))
            def _():
                chain(l, i - lag)

            @pl.when(i < NT)
            def _():
                intra(l, i)

            return carry

        lax.fori_loop(0, 2 * NT, b_step, 0)

        sq[...] = jnp.zeros((TOK, 128), F32)

        def d_step(i, carry):
            @pl.when(i >= HALF)
            def _():
                x_arrival(l, 2 * (i - HALF)).wait_recv()
                x_arrival(l, 2 * (i - HALF) + 1).wait_recv()

            tile = lax.rem(i + HALF * k, NT)
            cols = pl.ds(pl.multiple_of(tile * TILE, TILE), TILE)
            g = g1[:, cols] + g2[:, cols] * mm(cmat_s[l], x_s[l, tile])
            g1[:, cols] = g
            g = g * g
            sq[...] += g[:, :128] + g[:, 128:]
            return carry

        lax.fori_loop(0, NT, d_step, 0)

        hi, lo = parts(sq[...], 2)
        ones = jnp.ones((16, 128), BF16)
        total = (mm_nt(ones, hi.astype(BF16)) + mm_nt(ones, lo.astype(BF16)))[0:8]
        ps_s[l] = total
        for d in range(1, n_tp):
            p_copy(l, d).start()
        for d in range(1, n_tp):
            p_copy(l, d).wait_recv()
            total = total + ps_r[l, d - 1]
        scale = lax.rsqrt(total[0:1] / (CH * n_tp) + 1e-05)
        r_s[...] = jnp.broadcast_to(scale, (128, TOK)).T

        def e_step(i, carry):
            row = TOK - 32 * (i + 1)
            rows = pl.ds(pl.multiple_of(row, 32), 32)
            ext = pl.ds(pl.multiple_of(BLK + row, 32), 32)
            r = r_s[rows, :]
            for t in range(CH // 128):
                cols = pl.ds(t * 128, 128)
                gains = jnp.where(l == 0, gain[0, 0:1, cols], gain[0, 1:2, cols])
                uext[l + 1, ext, cols] = (
                    uext[l, ext, cols].astype(F32) + g1[rows, cols] * (gains * r)
                ).astype(BF16)

            @pl.when((l == 0) & (i == 0) & (c + 1 < n_ctx))
            def _():
                halo_copy(1).start()

            for n in range(ROUND):

                @pl.when((l == LAYERS - 1) & (i == n))
                def _():
                    round_copy(n, 0).start()

            @pl.when((l == LAYERS - 1) & (i >= ROUND))
            def _():
                o_copy(i).start()

            return carry

        lax.fori_loop(0, RC, e_step, 0)
        return carry

    lax.fori_loop(0, LAYERS, layer, 0)

    for hop in range(1, n_sec - 1):
        for n in range(ROUND):
            round_copy(n, hop - 1).wait_recv()
            round_copy(n, hop).start()

    @pl.when(c + 1 < n_ctx)
    def _():
        for cp in first_copies():
            cp.wait_send()
        for l in range(LAYERS):
            halo_copy(l).wait_send()

    def sent(n, carry):
        l, i = lax.div(n, HC), lax.rem(n, HC)

        @pl.when(lax.rem(i, 2) == 0)
        def _():
            l_copy(l, lax.div(i, 2)).wait_send()

        x_copy(l, i).wait_send()

        @pl.when(z < last_z)
        def _():
            s_copy(l, i).wait_send()

        return carry

    lax.fori_loop(0, LAYERS * HC, sent, 0)
    for l in range(LAYERS):
        for d in range(1, n_tp):
            p_copy(l, d).wait_send()

    def moved(i, carry):
        o_copy(i).wait_send()
        o_copy(i).wait_recv()
        return carry

    lax.fori_loop(ROUND, RC, moved, 0)
    for n in range(ROUND):
        for hop in range(n_sec - 1):
            round_copy(n, hop).wait_send()
        round_copy(n, n_sec - 2).wait_recv()


def hand_over(made, out, rows, sem):
    def part(n, way):
        at = pl.ds(32 * n, 32)
        if way == 0:
            return pltpu.make_async_copy(made.at[0, at], rows.at[at], sem.at[0, n])
        return pltpu.make_async_copy(rows.at[at], out.at[0, at], sem.at[1, n])

    for n in range(RC):
        part(n, 0).start()
    for n in range(RC):
        part(n, 0).wait()
        part(n, 1).start()
    for n in range(RC):
        part(n, 1).wait()


def per_device(sizes, *args):
    hbm = pl.BlockSpec(memory_space=pltpu.HBM)
    dma = pltpu.SemaphoreType.DMA
    n_sec, _, n_tp = sizes
    made = pl.pallas_call(
        functools.partial(kernel, *sizes),
        out_shape=jax.ShapeDtypeStruct((1, TOK, CH), BF16),
        in_specs=[hbm] * len(args),
        out_specs=hbm,
        scratch_shapes=[
            pltpu.VMEM((1, LAYERS, 32, TOK), F32),
            pltpu.VMEM((1, LAYERS, 32, TOK), F32),
            pltpu.VMEM((1, TOK), jnp.int32),
            pltpu.VMEM((1, LAYERS, 4, CH), F32),
            pltpu.VMEM((1, LAYERS, 4, 2, 128), F32),
            pltpu.SMEM((1, LAYERS, 32), F32),
            pltpu.VMEM((1, LAYERS, CH), F32),
            pltpu.VMEM((LAYERS + 1, BLK + TOK, CH), BF16),
            pltpu.VMEM((LAYERS, BLK + TOK, 256), BF16),
            pltpu.VMEM((1, TOK), jnp.int32),
            pltpu.VMEM((LAYERS, TOK, CH), BF16),
            pltpu.VMEM((2, 3 * BLK, 256), BF16),
            pltpu.VMEM((128, CH), BF16),
            pltpu.VMEM((128, CH), BF16),
            pltpu.VMEM((128, 4096), BF16),
            pltpu.VMEM((LAYERS, TOK, 128), BF16),
            pltpu.VMEM((LAYERS, TOK, 128), BF16),
            pltpu.VMEM((LAYERS, TOK, 128), BF16),
            pltpu.VMEM((LAYERS, NT, 8, TOK), F32),
            pltpu.VMEM((LAYERS, TOK, 128), BF16),
            pltpu.VMEM((LAYERS, 128, TOK), BF16),
            pltpu.VMEM((LAYERS, 2, BLK, BLK), F32),
            pltpu.VMEM((TOK, CH), BF16),
            pltpu.VMEM((TOK, CH), BF16),
            pltpu.VMEM((NT, 128, TILE), BF16),
            pltpu.VMEM((LAYERS, NT, 144, TILE), BF16),
            pltpu.VMEM((LAYERS, HALF, 144, TILE), BF16),
            pltpu.VMEM((LAYERS, HC, 128, 128), BF16),
            pltpu.VMEM((LAYERS, HC, 128, 128), BF16),
            pltpu.VMEM((LAYERS, NT, 128, TILE), BF16),
            pltpu.VMEM((LAYERS, HC, 128, 128), BF16),
            pltpu.VMEM((TOK, CH), F32),
            pltpu.VMEM((TOK, CH), F32),
            pltpu.VMEM((TOK, 128), F32),
            pltpu.VMEM((LAYERS, 8, TOK), F32),
            pltpu.VMEM((LAYERS, max(n_tp - 1, 1), 8, TOK), F32),
            pltpu.VMEM((TOK, 128), F32),
            dma((14,)),
            dma((2, LAYERS)),
            dma((2, 2)),
            dma((2, LAYERS, HALF)),
            dma((2, LAYERS, HC)),
            dma((2, LAYERS, HC)),
            dma((2, LAYERS, max(n_tp - 1, 1))),
            dma((2, RC)),
            dma((2, n_sec - 1, ROUND)),
            pltpu.VMEM((max(n_sec - 2, 1), ROUND, 32, CH), BF16),
        ],
        compiler_params=pltpu.CompilerParams(
            collective_id=0, has_side_effects=True, vmem_limit_bytes=60 * 1024 * 1024
        ),
        cost_estimate=pl.CostEstimate(
            flops=2_000_000_000, bytes_accessed=6_000_000, transcendentals=6_000_000
        ),
        name="mixer",
    )(*args)
    return pl.pallas_call(
        hand_over,
        out_shape=jax.ShapeDtypeStruct((1, TOK, CH), BF16),
        in_specs=[pl.BlockSpec(memory_space=pl.ANY)],
        out_specs=pl.BlockSpec(memory_space=pl.ANY),
        scratch_shapes=[pltpu.VMEM((TOK, CH), BF16), dma((2, RC))],
        name="hand_over",
        compiler_params=pltpu.CompilerParams(vmem_limit_bytes=60 * 1024 * 1024),
    )(made)


def solution(mesh):
    in_specs = (
        P("section", "ctx", "tp"),
        P("section", None, "ctx", "tp"),
        P("section", None, None, "ctx", "tp"),
        P("section", None, "tp", "ctx"),
        P("section", None, "tp", "ctx"),
        P("section", "ctx"),
        P("section", None, None, "tp"),
        P("section", None, None, None, "tp"),
        P("section", None, "tp"),
        P("section", None, "tp"),
    )
    out_specs = P("section", "ctx", "tp")
    sizes = tuple(mesh.shape[a] for a in ("section", "ctx", "tp"))
    return jax.shard_map(
        functools.partial(per_device, sizes),
        mesh=mesh,
        in_specs=in_specs,
        out_specs=out_specs,
        check_vma=False,
    )
```

```python
import functools

import jax
import jax.numpy as jnp
from jax import lax
from jax.experimental import pallas as pl
from jax.experimental.pallas import tpu as pltpu
from jax.sharding import PartitionSpec as P

HDIM = 64
BLK = 128
TOK = 256
CH = 2048
TILE = 256
NT = CH // TILE
HALF = NT // 2
HC = 2 * HALF
RC = TOK // 32
ROUND = RC // 4
LAG = 4
LAYERS = 2
F32 = jnp.float32
BF16 = jnp.bfloat16
MESH = pl.DeviceIdType.MESH


def mm(a, b):
    return jnp.dot(a, b, preferred_element_type=F32)


def mm_nt(a, b):
    return lax.dot_general(a, b, (((1,), (1,)), ((), ())), preferred_element_type=F32)


def iota(shape, dim):
    return lax.broadcasted_iota(jnp.int32, shape, dim)


def parts(v, count):
    out = []
    for _ in range(count - 1):
        p = v.astype(BF16).astype(F32)
        out.append(p)
        v = v - p
    out.append(v)
    return out


def silu_of_half(h):
    return h + h * jnp.tanh(h)


def kernel(
    n_sec,
    n_ctx,
    n_tp,
    hid,
    gate,
    proj,
    step_h,
    decay_h,
    ids_h,
    cw_h,
    sw_h,
    skip_h,
    gain_h,
    out,
    step,
    decay,
    ids,
    cw,
    sw,
    skip,
    gain,
    uext,
    pext,
    idp,
    gbuf,
    same_s,
    e2a,
    e2b,
    ctf,
    cum_f,
    va,
    vb,
    cum_s,
    cmat_s,
    bt_s,
    sc_s,
    xs_s,
    dx_s,
    bs0_s,
    l_s,
    l_r,
    sin_s,
    sout_s,
    x_s,
    xo_s,
    g1,
    g2,
    sq,
    ps_s,
    ps_r,
    r_s,
    in_sem,
    halo_sem,
    first_sem,
    l_sem,
    s_sem,
    x_sem,
    p_sem,
    o_sem,
    r_sem,
    relay,
):
    sec = lax.axis_index("section")
    c = lax.axis_index("ctx")
    tp = lax.axis_index("tp")
    z = lax.div(c, 2)
    k = lax.rem(c, 2)
    last_z = n_ctx // 2 - 1
    partner = c + 1 - 2 * k
    core0 = k == 0

    in_small = []
    for n, (src, dst) in enumerate(
        [
            (ids_h, ids),
            (decay_h, decay),
            (step_h, step),
            (sw_h, sw),
            (cw_h, cw),
            (skip_h, skip),
            (gain_h, gain),
        ]
    ):
        cp = pltpu.make_async_copy(src, dst, in_sem.at[7 + n])
        cp.start()
        in_small.append(cp)
    in_hid = pltpu.make_async_copy(hid.at[0], uext.at[0, pl.ds(BLK, TOK)], in_sem.at[0])
    in_hid.start()
    in_proj = []
    for l in range(LAYERS):
        for w in range(2):
            cp = pltpu.make_async_copy(
                proj.at[0, l, w],
                pext.at[l, pl.ds(BLK, TOK), pl.ds(w * 128, 128)],
                in_sem.at[1 + 2 * l + w],
            )
            cp.start()
            in_proj.append(cp)
    in_gate = [
        pltpu.make_async_copy(gate.at[0, l], gbuf.at[l], in_sem.at[5 + l]) for l in range(LAYERS)
    ]

    @pl.when(c == 0)
    def _():
        for l in range(LAYERS):
            uext[l, pl.ds(112, 16), :] = jnp.zeros((16, CH), BF16)
            pext[l, pl.ds(112, 16), :] = jnp.zeros((16, 256), BF16)
        idp[...] = jnp.full((1, TOK), -1, jnp.int32)

    @pl.when(z == 0)
    def _():
        sin_s[...] = jnp.zeros(sin_s.shape, BF16)

    bar = pltpu.get_barrier_semaphore()

    def greet(**where):
        pl.semaphore_signal(bar, inc=1, device_id=where, device_id_type=MESH)

    @pl.when(c >= 1)
    def _():
        greet(ctx=c - 1)

    @pl.when(c >= 2)
    def _():
        greet(ctx=c - 2)

    @pl.when(core0)
    def _():
        greet(ctx=c + 1)

    for d in range(1, n_tp):
        greet(tp=lax.rem(tp + d, n_tp))
    greet(section=lax.rem(sec + n_sec - 1, n_sec))
    if n_sec > 2:
        greet(section=lax.rem(sec + 1, n_sec))

    q = iota((128, CH), 0)
    head = iota((128, CH), 1) // HDIM
    e2a[...] = jnp.where((q < 64) & (q % 32 == head), 1.0, 0.0).astype(BF16)
    e2b[...] = jnp.where((q >= 64) & (q % 32 == head), 1.0, 0.0).astype(BF16)
    for l in range(LAYERS):
        uext[l, pl.ds(0, 112), :] = jnp.zeros((112, CH), BF16)
        pext[l, pl.ds(0, 112), :] = jnp.zeros((112, 256), BF16)

    in_hid.wait()
    for cp in in_proj + in_small:
        cp.wait()
    for cp in in_gate:
        cp.start()

    greeted = (
        jnp.where(c + 1 < n_ctx, 1, 0) + jnp.where(c + 2 < n_ctx, 1, 0) + k + (n_tp - 1) + min(n_sec - 1, 2)
    )
    pl.semaphore_wait(bar, greeted)

    def halo_copy(l):
        return pltpu.make_async_remote_copy(
            src_ref=uext.at[l, pl.ds(BLK + TOK - 16, 16)],
            dst_ref=uext.at[l, pl.ds(112, 16)],
            send_sem=halo_sem.at[0, l],
            recv_sem=halo_sem.at[1, l],
            device_id={"ctx": c + 1},
            device_id_type=MESH,
        )

    def first_copies():
        return [
            pltpu.make_async_remote_copy(
                src_ref=ids,
                dst_ref=idp,
                send_sem=first_sem.at[0, 0],
                recv_sem=first_sem.at[1, 0],
                device_id={"ctx": c + 1},
                device_id_type=MESH,
            ),
            pltpu.make_async_remote_copy(
                src_ref=pext.at[:, pl.ds(BLK + TOK - 16, 16)],
                dst_ref=pext.at[:, pl.ds(112, 16)],
                send_sem=first_sem.at[0, 1],
                recv_sem=first_sem.at[1, 1],
                device_id={"ctx": c + 1},
                device_id_type=MESH,
            ),
        ]

    @pl.when(c + 1 < n_ctx)
    def _():
        for cp in first_copies():
            cp.start()
        halo_copy(0).start()

    m_row = ids[...].astype(F32)
    m_e0 = m_row[:, 127:128]
    m_e1 = m_row[:, 255:256]
    lane = iota((32, TOK), 1)

    def prep_decay(l):
        d3 = jnp.concatenate(parts(decay[0, l], 3), axis=0).astype(BF16)
        tri = jnp.where(iota((TOK, TOK), 0) <= iota((TOK, TOK), 1), 1.0, 0.0).astype(BF16)
        c3 = mm(d3, tri)
        cum = c3[0:32] + c3[32:64] + c3[64:96]
        for j in range(NT):
            cum_s[l, j, 0:4, :] = cum[4 * j : 4 * j + 4]
        cum_f[l] = cum
        cols = jnp.concatenate([cum, jnp.zeros((96, TOK), F32)], axis=0).T
        for j in range(NT):
            ctf[l, j] = pltpu.roll(cols, (128 - 4 * j) % 128, 1) if j else cols
        tot0 = cum[:, 127:128]
        tot1 = cum[:, 255:256]
        first = lane < BLK
        m_e = jnp.where(first[0:1], m_e0, m_e1)
        tail = jnp.where(first, tot0, tot1) - cum
        dt = step[0, l]
        w = dt * jnp.where(m_row == m_e, jnp.exp(jnp.minimum(tail, 0.0)), 0.0)
        va[l] = jnp.concatenate(parts(dt, 2) + parts(w, 2), axis=0).T.astype(BF16)

    prep_decay(0)

    @pl.when(c >= 1)
    def _():
        for cp in first_copies():
            cp.wait_recv()

    m_old = idp[...].astype(F32)
    m_ext = jnp.concatenate([m_old[:, 128:], m_row], axis=1)
    m_prev = m_old[:, 255:256]
    m_col = jnp.broadcast_to(m_row, (128, TOK)).T
    m_ext = jnp.broadcast_to(m_ext, (8, BLK + TOK))
    for j in range(3):
        back = pltpu.roll(m_ext, j + 1, 1)[0:1, BLK:]
        same = jnp.where(back == m_row, 1.0, 0.0)
        same_s[j] = jnp.broadcast_to(same, (128, TOK)).T


    def conv(u, b, taps):
        h = taps[3] * u[16:]
        for j in range(3):
            same = same_s[j, pl.ds(b * BLK, BLK), :]
            same = jnp.concatenate([same, same], axis=1)
            h = h + taps[2 - j] * (same * pltpu.roll(u, j + 1, 0)[16:])
        return h

    def prep(l):
        for b in range(2):
            rows = pl.ds(b * BLK, BLK)
            u = pext[l, pl.ds(b * BLK + 112, BLK + 16), :].astype(F32)
            taps = [
                0.5 * jnp.concatenate([sw[0, l, t, 0:1, :], sw[0, l, t, 1:2, :]], axis=1)
                for t in range(4)
            ]
            v = silu_of_half(conv(u, b, taps))
            bm = v[:, :128]
            cm = v[:, 128:].astype(BF16)
            cmat_s[l, rows, :] = cm
            bt_s[l, :, rows] = bm.T.astype(BF16)
            scores = mm_nt(cm, bm.astype(BF16))
            ok = (iota((BLK, BLK), 0) >= iota((BLK, BLK), 1)) & (
                m_col[b * BLK : (b + 1) * BLK] == m_row[:, b * BLK : (b + 1) * BLK]
            )
            sc_s[l, b] = jnp.where(ok, scores, 0.0)
        cum = cum_f[l]
        tot0 = cum[:, 127:128]
        first = lane < BLK
        f = jnp.where(m_row == m_prev, jnp.exp(jnp.minimum(cum, 0.0)), 0.0)
        f1 = jnp.where(
            (m_row == m_e0) & jnp.logical_not(first), jnp.exp(jnp.minimum(cum - tot0, 0.0)), 0.0
        )
        vb[l] = jnp.concatenate(parts(f, 2) + parts(f1, 2), axis=0).T.astype(BF16)

    prep(0)

    def l_copy(l, i):
        return pltpu.make_async_remote_copy(
            src_ref=l_s.at[l, HALF * (1 - k) + i],
            dst_ref=l_r.at[l, i],
            send_sem=l_sem.at[0, l, i],
            recv_sem=l_sem.at[1, l, i],
            device_id={"ctx": partner},
            device_id_type=MESH,
        )

    def s_copy(l, i):
        return pltpu.make_async_remote_copy(
            src_ref=sout_s.at[l, i],
            dst_ref=sin_s.at[l, i],
            send_sem=s_sem.at[0, l, i],
            recv_sem=s_sem.at[1, l, i],
            device_id={"ctx": c + 2},
            device_id_type=MESH,
        )

    def half_tile(i):
        return pl.ds(pl.multiple_of(lax.rem(i, 2) * 128, 128), 128)

    def x_copy(l, i):
        return pltpu.make_async_remote_copy(
            src_ref=xo_s.at[l, i],
            dst_ref=x_s.at[l, HALF * k + lax.div(i, 2), :, half_tile(i)],
            send_sem=x_sem.at[0, l, i],
            recv_sem=x_sem.at[1, l, i],
            device_id={"ctx": partner},
            device_id_type=MESH,
        )

    def x_arrival(l, i):
        return pltpu.make_async_remote_copy(
            src_ref=xo_s.at[l, i],
            dst_ref=x_s.at[l, HALF * (1 - k) + lax.div(i, 2), :, half_tile(i)],
            send_sem=x_sem.at[0, l, i],
            recv_sem=x_sem.at[1, l, i],
            device_id={"ctx": partner},
            device_id_type=MESH,
        )

    def p_copy(l, d):
        return pltpu.make_async_remote_copy(
            src_ref=ps_s.at[l],
            dst_ref=ps_r.at[l, d - 1],
            send_sem=p_sem.at[0, l, d - 1],
            recv_sem=p_sem.at[1, l, d - 1],
            device_id={"tp": lax.rem(tp + d, n_tp)},
            device_id_type=MESH,
        )

    def o_copy(i):
        row = TOK - 32 * (i + 1)
        return pltpu.make_async_remote_copy(
            src_ref=uext.at[LAYERS, pl.ds(pl.multiple_of(BLK + row, 32), 32)],
            dst_ref=out.at[0, pl.ds(pl.multiple_of(row, 32), 32)],
            send_sem=o_sem.at[0, i],
            recv_sem=o_sem.at[1, i],
            device_id={"section": lax.rem(sec + 1, n_sec)},
            device_id_type=MESH,
        )

    def round_copy(i, hop):
        row = TOK - 32 * (i + 1)
        return pltpu.make_async_remote_copy(
            src_ref=uext.at[LAYERS, pl.ds(BLK + row, 32)] if hop == 0 else relay.at[hop - 1, i],
            dst_ref=out.at[0, pl.ds(row, 32)] if hop == n_sec - 2 else relay.at[hop, i],
            send_sem=r_sem.at[0, hop, i],
            recv_sem=r_sem.at[1, hop, i],
            device_id={"section": lax.rem(sec + n_sec - 1, n_sec)},
            device_id_type=MESH,
        )

    def local_part(l, i):
        tile = lax.rem(i + HALF * (1 - k), NT)
        cols = pl.ds(pl.multiple_of(tile * TILE, TILE), TILE)
        taps = [0.5 * cw[0, l, pl.ds(t, 1), cols] for t in range(4)]
        ea, eb = e2a[:, cols], e2b[:, cols]
        sums = []
        for b in range(2):
            rows = pl.ds(b * BLK, BLK)
            u = uext[l, pl.ds(b * BLK + 112, BLK + 16), cols].astype(F32)
            xs = silu_of_half(conv(u, b, taps)).astype(BF16)
            xs_s[rows, cols] = xs
            xs = xs.astype(F32)
            v = va[l, rows, :]
            dx_s[rows, cols] = (mm(v, ea) * xs).astype(BF16)
            sums.append(mm(bt_s[l, :, rows], (mm(v, eb) * xs).astype(BF16)))
        vend = vb[l, pl.ds(TOK - 16, 16), :]
        d_all = mm(vend, ea)[15:16]
        d_blk = mm(vend, eb)[15:16]
        bs0_s[tile] = sums[0].astype(BF16)
        l_s[l, tile, pl.ds(0, 128), :] = (d_blk * sums[0] + sums[1]).astype(BF16)
        hi, lo = parts(d_all, 2)
        row = iota((16, TILE), 0)
        l_s[l, tile, pl.ds(128, 16), :] = jnp.where(
            row == 0, hi, jnp.where(row == 1, lo, 0.0)
        ).astype(BF16)

    def chain(l, i):
        @pl.when(lax.rem(i, 2) == 0)
        def _():
            l_copy(l, lax.div(i, 2)).wait_recv()

        @pl.when(z > 0)
        def _():
            s_copy(l, i).wait_recv()

        tile = HALF * k + lax.div(i, 2)
        lanes = half_tile(i)

        def both(ref):
            d = ref[pl.ds(128, 16), lanes].astype(F32)
            return ref[pl.ds(0, 128), lanes].astype(F32), d[0:1] + d[1:2]

        mine, d_mine = both(l_s.at[l, tile])
        other, d_other = both(l_r.at[l, lax.div(i, 2)])
        s = sin_s[l, i].astype(F32)
        x1 = jnp.where(core0, mine, other) + jnp.where(core0, d_mine, d_other) * s
        end = jnp.where(core0, other, mine) + jnp.where(core0, d_other, d_mine) * x1
        sout_s[l, i] = end.astype(BF16)

        @pl.when(z < last_z)
        def _():
            s_copy(l, i).start()

        x_s[l, tile, :, lanes] = jnp.where(core0, s, x1).astype(BF16)
        xo_s[l, i] = jnp.where(core0, x1, s).astype(BF16)
        x_copy(l, i).start()

    low = iota((BLK, 128), 1) < HDIM
    low_row = iota((1, 128), 1) < HDIM

    def intra(l, tile):
        cols = pl.ds(pl.multiple_of(tile * TILE, TILE), TILE)
        for b in range(2):
            rows = pl.ds(b * BLK, BLK)
            scores = sc_s[l, b]
            decays = ctf[l, tile, rows, :]
            ys = []
            for p in range(2):
                h0 = 4 * tile + 2 * p
                pair = pl.ds(pl.multiple_of(tile * TILE + p * 128, 128), 128)
                mix = []
                for o in range(2):
                    q = 2 * p + o
                    gap = decays[:, q : q + 1] - cum_s[l, tile, 2 * p + o : 2 * p + o + 1, rows]
                    mix.append((scores * jnp.exp(jnp.minimum(gap, 0.0))).astype(BF16))
                dx = dx_s[rows, pair].astype(F32)
                both = jnp.concatenate(
                    [jnp.where(low, dx, 0.0), jnp.where(low, 0.0, dx)], axis=0
                ).astype(BF16)
                y = mm(jnp.concatenate(mix, axis=1), both)
                gains = jnp.where(low_row, skip[0, l, h0], skip[0, l, h0 + 1])
                ys.append(y + gains * xs_s[rows, pair].astype(F32))
            y = jnp.concatenate(ys, axis=1)
            v = vb[l, rows, :]
            if b == 1:
                y = y + mm(v, e2b[:, cols]) * mm(cmat_s[l, rows, :], bs0_s[tile])
            h = 0.5 * gbuf[l, rows, cols].astype(F32)
            sg = silu_of_half(h)
            g1[rows, cols] = y * sg
            g2[rows, cols] = mm(v, e2a[:, cols]) * sg

    def layer(l, carry):
        @pl.when(c >= 1)
        def _():
            halo_copy(l).wait_recv()

        def a_step(i, carry):
            local_part(l, i)

            @pl.when(i < HALF)
            def _():
                l_copy(l, i).start()

            return carry

        lax.fori_loop(0, NT, a_step, 0)

        @pl.when(l == 0)
        def _():
            for cp in in_gate:
                cp.wait()

        lag = jnp.where(l == 0, jnp.minimum(LAG * z, NT), 0)
        prep_at = jnp.where(z <= 2, 2 * NT - 1, NT)

        def b_step(i, carry):
            @pl.when((l == 0) & (i == prep_at))
            def _():
                prep_decay(1)
                prep(1)

            @pl.when((i >= lag) & (i < lag + HC))
            def _():
                chain(l, i - lag)

            @pl.when(i < NT)
            def _():
                intra(l, i)

            return carry

        lax.fori_loop(0, 2 * NT, b_step, 0)

        sq[...] = jnp.zeros((TOK, 128), F32)

        def d_step(i, carry):
            @pl.when(i >= HALF)
            def _():
                x_arrival(l, 2 * (i - HALF)).wait_recv()
                x_arrival(l, 2 * (i - HALF) + 1).wait_recv()

            tile = lax.rem(i + HALF * k, NT)
            cols = pl.ds(pl.multiple_of(tile * TILE, TILE), TILE)
            g = g1[:, cols] + g2[:, cols] * mm(cmat_s[l], x_s[l, tile])
            g1[:, cols] = g
            g = g * g
            sq[...] += g[:, :128] + g[:, 128:]
            return carry

        lax.fori_loop(0, NT, d_step, 0)

        hi, lo = parts(sq[...], 2)
        ones = jnp.ones((16, 128), BF16)
        total = (mm_nt(ones, hi.astype(BF16)) + mm_nt(ones, lo.astype(BF16)))[0:8]
        ps_s[l] = total
        for d in range(1, n_tp):
            p_copy(l, d).start()
        for d in range(1, n_tp):
            p_copy(l, d).wait_recv()
            total = total + ps_r[l, d - 1]
        scale = lax.rsqrt(total[0:1] / (CH * n_tp) + 1e-05)
        r_s[...] = jnp.broadcast_to(scale, (128, TOK)).T

        def e_step(i, carry):
            row = TOK - 32 * (i + 1)
            rows = pl.ds(pl.multiple_of(row, 32), 32)
            ext = pl.ds(pl.multiple_of(BLK + row, 32), 32)
            r = r_s[rows, :]
            for t in range(CH // 128):
                cols = pl.ds(t * 128, 128)
                gains = jnp.where(l == 0, gain[0, 0:1, cols], gain[0, 1:2, cols])
                uext[l + 1, ext, cols] = (
                    uext[l, ext, cols].astype(F32) + g1[rows, cols] * (gains * r)
                ).astype(BF16)

            @pl.when((l == 0) & (i == 0) & (c + 1 < n_ctx))
            def _():
                halo_copy(1).start()

            for n in range(ROUND):

                @pl.when((l == LAYERS - 1) & (i == n))
                def _():
                    round_copy(n, 0).start()

            @pl.when((l == LAYERS - 1) & (i >= ROUND))
            def _():
                o_copy(i).start()

            return carry

        lax.fori_loop(0, RC, e_step, 0)
        return carry

    lax.fori_loop(0, LAYERS, layer, 0)

    for hop in range(1, n_sec - 1):
        for n in range(ROUND):
            round_copy(n, hop - 1).wait_recv()
            round_copy(n, hop).start()

    @pl.when(c + 1 < n_ctx)
    def _():
        for cp in first_copies():
            cp.wait_send()
        for l in range(LAYERS):
            halo_copy(l).wait_send()

    def sent(n, carry):
        l, i = lax.div(n, HC), lax.rem(n, HC)

        @pl.when(lax.rem(i, 2) == 0)
        def _():
            l_copy(l, lax.div(i, 2)).wait_send()

        x_copy(l, i).wait_send()

        @pl.when(z < last_z)
        def _():
            s_copy(l, i).wait_send()

        return carry

    lax.fori_loop(0, LAYERS * HC, sent, 0)
    for l in range(LAYERS):
        for d in range(1, n_tp):
            p_copy(l, d).wait_send()

    def moved(i, carry):
        o_copy(i).wait_send()
        o_copy(i).wait_recv()
        return carry

    lax.fori_loop(ROUND, RC, moved, 0)
    for n in range(ROUND):
        for hop in range(n_sec - 1):
            round_copy(n, hop).wait_send()
        round_copy(n, n_sec - 2).wait_recv()


def hand_over(made, out, rows, sem):
    def part(n, way):
        at = pl.ds(32 * n, 32)
        if way == 0:
            return pltpu.make_async_copy(made.at[0, at], rows.at[at], sem.at[0, n])
        return pltpu.make_async_copy(rows.at[at], out.at[0, at], sem.at[1, n])

    for n in range(RC):
        part(n, 0).start()
    for n in range(RC):
        part(n, 0).wait()
        part(n, 1).start()
    for n in range(RC):
        part(n, 1).wait()


def per_device(sizes, *args):
    hbm = pl.BlockSpec(memory_space=pltpu.HBM)
    dma = pltpu.SemaphoreType.DMA
    n_sec, _, n_tp = sizes
    made = pl.pallas_call(
        functools.partial(kernel, *sizes),
        out_shape=jax.ShapeDtypeStruct((1, TOK, CH), BF16),
        in_specs=[hbm] * len(args),
        out_specs=hbm,
        scratch_shapes=[
            pltpu.VMEM((1, LAYERS, 32, TOK), F32),
            pltpu.VMEM((1, LAYERS, 32, TOK), F32),
            pltpu.VMEM((1, TOK), jnp.int32),
            pltpu.VMEM((1, LAYERS, 4, CH), F32),
            pltpu.VMEM((1, LAYERS, 4, 2, 128), F32),
            pltpu.SMEM((1, LAYERS, 32), F32),
            pltpu.VMEM((1, LAYERS, CH), F32),
            pltpu.VMEM((LAYERS + 1, BLK + TOK, CH), BF16),
            pltpu.VMEM((LAYERS, BLK + TOK, 256), BF16),
            pltpu.VMEM((1, TOK), jnp.int32),
            pltpu.VMEM((LAYERS, TOK, CH), BF16),
            pltpu.VMEM((3, TOK, 128), F32),
            pltpu.VMEM((128, CH), BF16),
            pltpu.VMEM((128, CH), BF16),
            pltpu.VMEM((LAYERS, NT, TOK, 128), F32),
            pltpu.VMEM((LAYERS, 32, TOK), F32),
            pltpu.VMEM((LAYERS, TOK, 128), BF16),
            pltpu.VMEM((LAYERS, TOK, 128), BF16),
            pltpu.VMEM((LAYERS, NT, 8, TOK), F32),
            pltpu.VMEM((LAYERS, TOK, 128), BF16),
            pltpu.VMEM((LAYERS, 128, TOK), BF16),
            pltpu.VMEM((LAYERS, 2, BLK, BLK), F32),
            pltpu.VMEM((TOK, CH), BF16),
            pltpu.VMEM((TOK, CH), BF16),
            pltpu.VMEM((NT, 128, TILE), BF16),
            pltpu.VMEM((LAYERS, NT, 144, TILE), BF16),
            pltpu.VMEM((LAYERS, HALF, 144, TILE), BF16),
            pltpu.VMEM((LAYERS, HC, 128, 128), BF16),
            pltpu.VMEM((LAYERS, HC, 128, 128), BF16),
            pltpu.VMEM((LAYERS, NT, 128, TILE), BF16),
            pltpu.VMEM((LAYERS, HC, 128, 128), BF16),
            pltpu.VMEM((TOK, CH), F32),
            pltpu.VMEM((TOK, CH), F32),
            pltpu.VMEM((TOK, 128), F32),
            pltpu.VMEM((LAYERS, 8, TOK), F32),
            pltpu.VMEM((LAYERS, max(n_tp - 1, 1), 8, TOK), F32),
            pltpu.VMEM((TOK, 128), F32),
            dma((14,)),
            dma((2, LAYERS)),
            dma((2, 2)),
            dma((2, LAYERS, HALF)),
            dma((2, LAYERS, HC)),
            dma((2, LAYERS, HC)),
            dma((2, LAYERS, max(n_tp - 1, 1))),
            dma((2, RC)),
            dma((2, n_sec - 1, ROUND)),
            pltpu.VMEM((max(n_sec - 2, 1), ROUND, 32, CH), BF16),
        ],
        compiler_params=pltpu.CompilerParams(
            collective_id=0, has_side_effects=True, vmem_limit_bytes=60 * 1024 * 1024
        ),
        cost_estimate=pl.CostEstimate(
            flops=2_000_000_000, bytes_accessed=6_000_000, transcendentals=6_000_000
        ),
        name="mixer",
    )(*args)
    return pl.pallas_call(
        hand_over,
        out_shape=jax.ShapeDtypeStruct((1, TOK, CH), BF16),
        in_specs=[pl.BlockSpec(memory_space=pl.ANY)],
        out_specs=pl.BlockSpec(memory_space=pl.ANY),
        scratch_shapes=[pltpu.VMEM((TOK, CH), BF16), dma((2, RC))],
        name="hand_over",
        compiler_params=pltpu.CompilerParams(vmem_limit_bytes=60 * 1024 * 1024),
    )(made)


def solution(mesh):
    in_specs = (
        P("section", "ctx", "tp"),
        P("section", None, "ctx", "tp"),
        P("section", None, None, "ctx", "tp"),
        P("section", None, "tp", "ctx"),
        P("section", None, "tp", "ctx"),
        P("section", "ctx"),
        P("section", None, None, "tp"),
        P("section", None, None, None, "tp"),
        P("section", None, "tp"),
        P("section", None, "tp"),
    )
    out_specs = P("section", "ctx", "tp")
    sizes = tuple(mesh.shape[a] for a in ("section", "ctx", "tp"))
    return jax.shard_map(
        functools.partial(per_device, sizes),
        mesh=mesh,
        in_specs=in_specs,
        out_specs=out_specs,
        check_vma=False,
    )
```

```python
import functools

import jax
import jax.numpy as jnp
from jax import lax
from jax.experimental import pallas as pl
from jax.experimental.pallas import tpu as pltpu
from jax.sharding import PartitionSpec as P

HDIM = 64
BLK = 128
TOK = 256
CH = 2048
TILE = 256
NT = CH // TILE
HALF = NT // 2
HC = 2 * HALF
RC = TOK // 32
ROUND = RC // 4
PART = CH // 2
LAG = 4
LAYERS = 2
F32 = jnp.float32
BF16 = jnp.bfloat16
MESH = pl.DeviceIdType.MESH


def mm(a, b):
    return jnp.dot(a, b, preferred_element_type=F32)


def mm_nt(a, b):
    return lax.dot_general(a, b, (((1,), (1,)), ((), ())), preferred_element_type=F32)


def iota(shape, dim):
    return lax.broadcasted_iota(jnp.int32, shape, dim)


def parts(v, count):
    out = []
    for _ in range(count - 1):
        p = v.astype(BF16).astype(F32)
        out.append(p)
        v = v - p
    out.append(v)
    return out


def silu_of_half(h):
    return h + h * jnp.tanh(h)


def kernel(
    n_sec,
    n_ctx,
    n_tp,
    hid,
    gate,
    proj,
    step_h,
    decay_h,
    ids_h,
    cw_h,
    sw_h,
    skip_h,
    gain_h,
    out,
    step,
    decay,
    ids,
    cw,
    sw,
    skip,
    gain,
    uext,
    pext,
    idp,
    gbuf,
    same_s,
    e2a,
    e2b,
    ctf,
    cum_f,
    va,
    vb,
    cum_s,
    cmat_s,
    bt_s,
    sc_s,
    xs_s,
    dx_s,
    bs0_s,
    l_s,
    l_r,
    sin_s,
    sout_s,
    x_s,
    xo_s,
    g1,
    g2,
    sq,
    ps_s,
    ps_r,
    r_s,
    in_sem,
    halo_sem,
    first_sem,
    l_sem,
    s_sem,
    x_sem,
    p_sem,
    o_sem,
    r_sem,
    relay,
    e_sem,
    out_sem,
    u_r,
    scale_s,
    scale_r,
    gated_s,
    gated_r,
    g_sem,
    relay_g,
):
    sec = lax.axis_index("section")
    c = lax.axis_index("ctx")
    tp = lax.axis_index("tp")
    z = lax.div(c, 2)
    k = lax.rem(c, 2)
    last_z = n_ctx // 2 - 1
    partner = c + 1 - 2 * k
    core0 = k == 0
    ahead = pl.ds(pl.multiple_of(k * PART, PART), PART)
    late = pl.ds(pl.multiple_of((1 - k) * PART, PART), PART)

    in_small = []
    for n, (src, dst) in enumerate(
        [
            (ids_h, ids),
            (decay_h, decay),
            (step_h, step),
            (sw_h, sw),
            (cw_h, cw),
            (skip_h, skip),
            (gain_h, gain),
        ]
    ):
        cp = pltpu.make_async_copy(src, dst, in_sem.at[7 + n])
        cp.start()
        in_small.append(cp)
    in_hid = pltpu.make_async_copy(hid.at[0], uext.at[0, pl.ds(BLK, TOK)], in_sem.at[0])
    in_hid.start()
    in_proj = []
    for l in range(LAYERS):
        for w in range(2):
            cp = pltpu.make_async_copy(
                proj.at[0, l, w],
                pext.at[l, pl.ds(BLK, TOK), pl.ds(w * 128, 128)],
                in_sem.at[1 + 2 * l + w],
            )
            cp.start()
            in_proj.append(cp)
    in_gate = [
        pltpu.make_async_copy(gate.at[0, l], gbuf.at[l], in_sem.at[5 + l]) for l in range(LAYERS)
    ]

    @pl.when(c == 0)
    def _():
        for l in range(LAYERS):
            uext[l, pl.ds(112, 16), :] = jnp.zeros((16, CH), BF16)
            pext[l, pl.ds(112, 16), :] = jnp.zeros((16, 256), BF16)
        idp[...] = jnp.full((1, TOK), -1, jnp.int32)

    @pl.when(z == 0)
    def _():
        sin_s[...] = jnp.zeros(sin_s.shape, BF16)

    bar = pltpu.get_barrier_semaphore()

    def greet(**where):
        pl.semaphore_signal(bar, inc=1, device_id=where, device_id_type=MESH)

    @pl.when(c >= 1)
    def _():
        greet(ctx=c - 1)

    @pl.when(c >= 2)
    def _():
        greet(ctx=c - 2)

    @pl.when(core0)
    def _():
        greet(ctx=c + 1)

    for d in range(1, n_tp):
        greet(tp=lax.rem(tp + d, n_tp))
    greet(section=lax.rem(sec + n_sec - 1, n_sec))
    if n_sec > 2:
        greet(section=lax.rem(sec + 1, n_sec))

    q = iota((128, CH), 0)
    head = iota((128, CH), 1) // HDIM
    e2a[...] = jnp.where((q < 64) & (q % 32 == head), 1.0, 0.0).astype(BF16)
    e2b[...] = jnp.where((q >= 64) & (q % 32 == head), 1.0, 0.0).astype(BF16)
    for l in range(LAYERS):
        uext[l, pl.ds(0, 112), :] = jnp.zeros((112, CH), BF16)
        pext[l, pl.ds(0, 112), :] = jnp.zeros((112, 256), BF16)

    in_hid.wait()
    for cp in in_proj + in_small:
        cp.wait()
    for cp in in_gate:
        cp.start()

    greeted = (
        jnp.where(c + 1 < n_ctx, 1, 0) + jnp.where(c + 2 < n_ctx, 1, 0) + k + (n_tp - 1) + min(n_sec - 1, 2)
    )
    pl.semaphore_wait(bar, greeted)

    def halo_copy(l):
        return pltpu.make_async_remote_copy(
            src_ref=uext.at[l, pl.ds(BLK + TOK - 16, 16)],
            dst_ref=uext.at[l, pl.ds(112, 16)],
            send_sem=halo_sem.at[0, l],
            recv_sem=halo_sem.at[1, l],
            device_id={"ctx": c + 1},
            device_id_type=MESH,
        )

    def first_copies():
        return [
            pltpu.make_async_remote_copy(
                src_ref=ids,
                dst_ref=idp,
                send_sem=first_sem.at[0, 0],
                recv_sem=first_sem.at[1, 0],
                device_id={"ctx": c + 1},
                device_id_type=MESH,
            ),
            pltpu.make_async_remote_copy(
                src_ref=pext.at[:, pl.ds(BLK + TOK - 16, 16)],
                dst_ref=pext.at[:, pl.ds(112, 16)],
                send_sem=first_sem.at[0, 1],
                recv_sem=first_sem.at[1, 1],
                device_id={"ctx": c + 1},
                device_id_type=MESH,
            ),
        ]

    @pl.when(c + 1 < n_ctx)
    def _():
        for cp in first_copies():
            cp.start()
        halo_copy(0).start()

    m_row = ids[...].astype(F32)
    m_e0 = m_row[:, 127:128]
    m_e1 = m_row[:, 255:256]
    lane = iota((32, TOK), 1)

    def prep_decay(l):
        d3 = jnp.concatenate(parts(decay[0, l], 3), axis=0).astype(BF16)
        tri = jnp.where(iota((TOK, TOK), 0) <= iota((TOK, TOK), 1), 1.0, 0.0).astype(BF16)
        c3 = mm(d3, tri)
        cum = c3[0:32] + c3[32:64] + c3[64:96]
        for j in range(NT):
            cum_s[l, j, 0:4, :] = cum[4 * j : 4 * j + 4]
        cum_f[l] = cum
        cols = jnp.concatenate([cum, jnp.zeros((96, TOK), F32)], axis=0).T
        for j in range(NT):
            ctf[l, j] = pltpu.roll(cols, (128 - 4 * j) % 128, 1) if j else cols
        tot0 = cum[:, 127:128]
        tot1 = cum[:, 255:256]
        first = lane < BLK
        m_e = jnp.where(first[0:1], m_e0, m_e1)
        tail = jnp.where(first, tot0, tot1) - cum
        dt = step[0, l]
        w = dt * jnp.where(m_row == m_e, jnp.exp(jnp.minimum(tail, 0.0)), 0.0)
        va[l] = jnp.concatenate(parts(dt, 2) + parts(w, 2), axis=0).T.astype(BF16)

    prep_decay(0)

    @pl.when(c >= 1)
    def _():
        for cp in first_copies():
            cp.wait_recv()

    m_old = idp[...].astype(F32)
    m_ext = jnp.concatenate([m_old[:, 128:], m_row], axis=1)
    m_prev = m_old[:, 255:256]
    m_col = jnp.broadcast_to(m_row, (128, TOK)).T
    m_ext = jnp.broadcast_to(m_ext, (8, BLK + TOK))
    for j in range(3):
        back = pltpu.roll(m_ext, j + 1, 1)[0:1, BLK:]
        same = jnp.where(back == m_row, 1.0, 0.0)
        same_s[j] = jnp.broadcast_to(same, (128, TOK)).T


    def conv(u, b, taps):
        h = taps[3] * u[16:]
        for j in range(3):
            same = same_s[j, pl.ds(b * BLK, BLK), :]
            same = jnp.concatenate([same, same], axis=1)
            h = h + taps[2 - j] * (same * pltpu.roll(u, j + 1, 0)[16:])
        return h

    def prep(l):
        for b in range(2):
            rows = pl.ds(b * BLK, BLK)
            u = pext[l, pl.ds(b * BLK + 112, BLK + 16), :].astype(F32)
            taps = [
                0.5 * jnp.concatenate([sw[0, l, t, 0:1, :], sw[0, l, t, 1:2, :]], axis=1)
                for t in range(4)
            ]
            v = silu_of_half(conv(u, b, taps))
            bm = v[:, :128]
            cm = v[:, 128:].astype(BF16)
            cmat_s[l, rows, :] = cm
            bt_s[l, :, rows] = bm.T.astype(BF16)
            scores = mm_nt(cm, bm.astype(BF16))
            ok = (iota((BLK, BLK), 0) >= iota((BLK, BLK), 1)) & (
                m_col[b * BLK : (b + 1) * BLK] == m_row[:, b * BLK : (b + 1) * BLK]
            )
            sc_s[l, b] = jnp.where(ok, scores, 0.0)
        cum = cum_f[l]
        tot0 = cum[:, 127:128]
        first = lane < BLK
        f = jnp.where(m_row == m_prev, jnp.exp(jnp.minimum(cum, 0.0)), 0.0)
        f1 = jnp.where(
            (m_row == m_e0) & jnp.logical_not(first), jnp.exp(jnp.minimum(cum - tot0, 0.0)), 0.0
        )
        vb[l] = jnp.concatenate(parts(f, 2) + parts(f1, 2), axis=0).T.astype(BF16)

    prep(0)

    def l_copy(l, i):
        return pltpu.make_async_remote_copy(
            src_ref=l_s.at[l, HALF * (1 - k) + i],
            dst_ref=l_r.at[l, i],
            send_sem=l_sem.at[0, l, i],
            recv_sem=l_sem.at[1, l, i],
            device_id={"ctx": partner},
            device_id_type=MESH,
        )

    def s_copy(l, i):
        return pltpu.make_async_remote_copy(
            src_ref=sout_s.at[l, i],
            dst_ref=sin_s.at[l, i],
            send_sem=s_sem.at[0, l, i],
            recv_sem=s_sem.at[1, l, i],
            device_id={"ctx": c + 2},
            device_id_type=MESH,
        )

    def half_tile(i):
        return pl.ds(pl.multiple_of(lax.rem(i, 2) * 128, 128), 128)

    def x_copy(l, i):
        return pltpu.make_async_remote_copy(
            src_ref=xo_s.at[l, i],
            dst_ref=x_s.at[l, HALF * k + lax.div(i, 2), :, half_tile(i)],
            send_sem=x_sem.at[0, l, i],
            recv_sem=x_sem.at[1, l, i],
            device_id={"ctx": partner},
            device_id_type=MESH,
        )

    def x_arrival(l, i):
        return pltpu.make_async_remote_copy(
            src_ref=xo_s.at[l, i],
            dst_ref=x_s.at[l, HALF * (1 - k) + lax.div(i, 2), :, half_tile(i)],
            send_sem=x_sem.at[0, l, i],
            recv_sem=x_sem.at[1, l, i],
            device_id={"ctx": partner},
            device_id_type=MESH,
        )

    def p_copy(l, d):
        return pltpu.make_async_remote_copy(
            src_ref=ps_s.at[l],
            dst_ref=ps_r.at[l, d - 1],
            send_sem=p_sem.at[0, l, d - 1],
            recv_sem=p_sem.at[1, l, d - 1],
            device_id={"tp": lax.rem(tp + d, n_tp)},
            device_id_type=MESH,
        )

    def o_copy(i):
        row = TOK - 32 * (i + 1)
        return pltpu.make_async_remote_copy(
            src_ref=uext.at[LAYERS, pl.ds(pl.multiple_of(BLK + row, 32), 32), late],
            dst_ref=out.at[0, pl.ds(pl.multiple_of(row, 32), 32), late],
            send_sem=o_sem.at[0, i],
            recv_sem=o_sem.at[1, i],
            device_id={"section": lax.rem(sec + 1, n_sec)},
            device_id_type=MESH,
        )

    def round_copy(i, hop):
        row = TOK - 32 * (i + 1)
        return pltpu.make_async_remote_copy(
            src_ref=uext.at[LAYERS, pl.ds(BLK + row, 32), late] if hop == 0 else relay.at[hop - 1, i],
            dst_ref=out.at[0, pl.ds(row, 32), late] if hop == n_sec - 2 else relay.at[hop, i],
            send_sem=r_sem.at[0, hop, i],
            recv_sem=r_sem.at[1, hop, i],
            device_id={"section": lax.rem(sec + n_sec - 1, n_sec)},
            device_id_type=MESH,
        )

    def next_copy(src, dst, n):
        return pltpu.make_async_remote_copy(
            src_ref=src,
            dst_ref=dst,
            send_sem=e_sem.at[0, n],
            recv_sem=e_sem.at[1, n],
            device_id={"section": lax.rem(sec + 1, n_sec)},
            device_id_type=MESH,
        )

    def stream_copy():
        return next_copy(uext.at[LAYERS - 1, pl.ds(BLK, TOK), ahead], u_r, 0)

    def scale_copy():
        return next_copy(scale_s, scale_r, 1)

    def gated_copy(i):
        return next_copy(gated_s.at[i], gated_r.at[i], 2 + i)

    def gated_round(hop):
        return pltpu.make_async_remote_copy(
            src_ref=gated_s.at[0] if hop == 0 else relay_g.at[hop - 1],
            dst_ref=gated_r.at[0] if hop == n_sec - 2 else relay_g.at[hop],
            send_sem=g_sem.at[0, hop],
            recv_sem=g_sem.at[1, hop],
            device_id={"section": lax.rem(sec + n_sec - 1, n_sec)},
            device_id_type=MESH,
        )

    def local_part(l, i):
        tile = lax.rem(i + HALF * (1 - k), NT)
        cols = pl.ds(pl.multiple_of(tile * TILE, TILE), TILE)
        taps = [0.5 * cw[0, l, pl.ds(t, 1), cols] for t in range(4)]
        ea, eb = e2a[:, cols], e2b[:, cols]
        sums = []
        for b in range(2):
            rows = pl.ds(b * BLK, BLK)
            u = uext[l, pl.ds(b * BLK + 112, BLK + 16), cols].astype(F32)
            xs = silu_of_half(conv(u, b, taps)).astype(BF16)
            xs_s[rows, cols] = xs
            xs = xs.astype(F32)
            v = va[l, rows, :]
            dx_s[rows, cols] = (mm(v, ea) * xs).astype(BF16)
            sums.append(mm(bt_s[l, :, rows], (mm(v, eb) * xs).astype(BF16)))
        vend = vb[l, pl.ds(TOK - 16, 16), :]
        d_all = mm(vend, ea)[15:16]
        d_blk = mm(vend, eb)[15:16]
        bs0_s[tile] = sums[0].astype(BF16)
        l_s[l, tile, pl.ds(0, 128), :] = (d_blk * sums[0] + sums[1]).astype(BF16)
        hi, lo = parts(d_all, 2)
        row = iota((16, TILE), 0)
        l_s[l, tile, pl.ds(128, 16), :] = jnp.where(
            row == 0, hi, jnp.where(row == 1, lo, 0.0)
        ).astype(BF16)

    def chain(l, i):
        @pl.when(lax.rem(i, 2) == 0)
        def _():
            l_copy(l, lax.div(i, 2)).wait_recv()

        @pl.when(z > 0)
        def _():
            s_copy(l, i).wait_recv()

        tile = HALF * k + lax.div(i, 2)
        lanes = half_tile(i)

        def both(ref):
            d = ref[pl.ds(128, 16), lanes].astype(F32)
            return ref[pl.ds(0, 128), lanes].astype(F32), d[0:1] + d[1:2]

        mine, d_mine = both(l_s.at[l, tile])
        other, d_other = both(l_r.at[l, lax.div(i, 2)])
        s = sin_s[l, i].astype(F32)
        x1 = jnp.where(core0, mine, other) + jnp.where(core0, d_mine, d_other) * s
        end = jnp.where(core0, other, mine) + jnp.where(core0, d_other, d_mine) * x1
        sout_s[l, i] = end.astype(BF16)

        @pl.when(z < last_z)
        def _():
            s_copy(l, i).start()

        x_s[l, tile, :, lanes] = jnp.where(core0, s, x1).astype(BF16)
        xo_s[l, i] = jnp.where(core0, x1, s).astype(BF16)
        x_copy(l, i).start()

    low = iota((BLK, 128), 1) < HDIM
    low_row = iota((1, 128), 1) < HDIM

    def intra(l, tile):
        cols = pl.ds(pl.multiple_of(tile * TILE, TILE), TILE)
        for b in range(2):
            rows = pl.ds(b * BLK, BLK)
            scores = sc_s[l, b]
            decays = ctf[l, tile, rows, :]
            ys = []
            for p in range(2):
                h0 = 4 * tile + 2 * p
                pair = pl.ds(pl.multiple_of(tile * TILE + p * 128, 128), 128)
                mix = []
                for o in range(2):
                    q = 2 * p + o
                    gap = decays[:, q : q + 1] - cum_s[l, tile, 2 * p + o : 2 * p + o + 1, rows]
                    mix.append((scores * jnp.exp(jnp.minimum(gap, 0.0))).astype(BF16))
                dx = dx_s[rows, pair].astype(F32)
                both = jnp.concatenate(
                    [jnp.where(low, dx, 0.0), jnp.where(low, 0.0, dx)], axis=0
                ).astype(BF16)
                y = mm(jnp.concatenate(mix, axis=1), both)
                gains = jnp.where(low_row, skip[0, l, h0], skip[0, l, h0 + 1])
                ys.append(y + gains * xs_s[rows, pair].astype(F32))
            y = jnp.concatenate(ys, axis=1)
            v = vb[l, rows, :]
            if b == 1:
                y = y + mm(v, e2b[:, cols]) * mm(cmat_s[l, rows, :], bs0_s[tile])
            h = 0.5 * gbuf[l, rows, cols].astype(F32)
            sg = silu_of_half(h)
            g1[rows, cols] = y * sg
            g2[rows, cols] = mm(v, e2a[:, cols]) * sg

    def layer(l, carry):
        @pl.when(c >= 1)
        def _():
            halo_copy(l).wait_recv()

        @pl.when(l == LAYERS - 1)
        def _():
            stream_copy().start()

        def a_step(i, carry):
            local_part(l, i)

            @pl.when(i < HALF)
            def _():
                l_copy(l, i).start()

            return carry

        lax.fori_loop(0, NT, a_step, 0)

        @pl.when(l == 0)
        def _():
            for cp in in_gate:
                cp.wait()

        lag = jnp.where(l == 0, jnp.minimum(LAG * z, NT), 0)
        prep_at = jnp.where(z <= 2, 2 * NT - 1, NT)

        def b_step(i, carry):
            @pl.when((l == 0) & (i == prep_at))
            def _():
                prep_decay(1)
                prep(1)

            @pl.when((i >= lag) & (i < lag + HC))
            def _():
                chain(l, i - lag)

            @pl.when(i < NT)
            def _():
                intra(l, i)

            return carry

        lax.fori_loop(0, 2 * NT, b_step, 0)

        sq[...] = jnp.zeros((TOK, 128), F32)

        def d_step(i, carry):
            @pl.when(i >= HALF)
            def _():
                x_arrival(l, 2 * (i - HALF)).wait_recv()
                x_arrival(l, 2 * (i - HALF) + 1).wait_recv()

            tile = lax.rem(i + HALF * k, NT)
            cols = pl.ds(pl.multiple_of(tile * TILE, TILE), TILE)
            g = g1[:, cols] + g2[:, cols] * mm(cmat_s[l], x_s[l, tile])
            g1[:, cols] = g

            @pl.when((l == LAYERS - 1) & (i < HALF))
            def _():
                gated_s[i] = (g * gain[0, LAYERS - 1 : LAYERS, cols]).astype(BF16)

                @pl.when(i == 0)
                def _():
                    gated_round(0).start()

                @pl.when(i > 0)
                def _():
                    gated_copy(i).start()

            g = g * g
            sq[...] += g[:, :128] + g[:, 128:]
            return carry

        lax.fori_loop(0, NT, d_step, 0)

        hi, lo = parts(sq[...], 2)
        ones = jnp.ones((16, 128), BF16)
        total = (mm_nt(ones, hi.astype(BF16)) + mm_nt(ones, lo.astype(BF16)))[0:8]
        ps_s[l] = total
        for d in range(1, n_tp):
            p_copy(l, d).start()
        for d in range(1, n_tp):
            p_copy(l, d).wait_recv()
            total = total + ps_r[l, d - 1]
        scale = lax.rsqrt(total[0:1] / (CH * n_tp) + 1e-05)
        r_s[...] = jnp.broadcast_to(scale, (128, TOK)).T

        @pl.when(l == LAYERS - 1)
        def _():
            scale_s[...] = jnp.broadcast_to(scale, (8, TOK))
            scale_copy().start()

        def e_step(i, carry):
            row = TOK - 32 * (i + 1)
            rows = pl.ds(pl.multiple_of(row, 32), 32)
            ext = pl.ds(pl.multiple_of(BLK + row, 32), 32)
            r = r_s[rows, :]

            def rows_of(start):
                for t in range(PART // 128):
                    cols = pl.ds(pl.multiple_of(start * PART + t * 128, 128), 128)
                    gains = jnp.where(l == 0, gain[0, 0:1, cols], gain[0, 1:2, cols])
                    uext[l + 1, ext, cols] = (
                        uext[l, ext, cols].astype(F32) + g1[rows, cols] * (gains * r)
                    ).astype(BF16)

            rows_of(1 - k)

            @pl.when(l < LAYERS - 1)
            def _():
                rows_of(k)

            @pl.when((l == 0) & (i == 0) & (c + 1 < n_ctx))
            def _():
                halo_copy(1).start()

            for n in range(ROUND):

                @pl.when((l == LAYERS - 1) & (i == n))
                def _():
                    round_copy(n, 0).start()

            @pl.when((l == LAYERS - 1) & (i >= ROUND))
            def _():
                o_copy(i).start()

            return carry

        lax.fori_loop(0, RC, e_step, 0)
        return carry

    lax.fori_loop(0, LAYERS, layer, 0)

    for hop in range(1, n_sec - 1):
        gated_round(hop - 1).wait_recv()
        gated_round(hop).start()
        for n in range(ROUND):
            round_copy(n, hop - 1).wait_recv()
            round_copy(n, hop).start()

    stream_copy().wait_recv()
    scale_copy().wait_recv()
    scale_col = jnp.broadcast_to(scale_r[0:1, :], (128, TOK)).T
    scale_col = jnp.concatenate([scale_col, scale_col], axis=1)

    def own_out(i):
        at = pl.ds(pl.multiple_of(k * PART + i * TILE, TILE), TILE)
        return pltpu.make_async_copy(gated_r.at[i], out.at[0, :, at], out_sem.at[i])

    for i in (1, 2, 3, 0):
        (gated_copy(i) if i else gated_round(n_sec - 2)).wait_recv()
        gated_r[i] = (
            u_r[:, i * TILE : (i + 1) * TILE].astype(F32) + gated_r[i].astype(F32) * scale_col
        ).astype(BF16)
        own_out(i).start()

    @pl.when(c + 1 < n_ctx)
    def _():
        for cp in first_copies():
            cp.wait_send()
        for l in range(LAYERS):
            halo_copy(l).wait_send()

    def sent(n, carry):
        l, i = lax.div(n, HC), lax.rem(n, HC)

        @pl.when(lax.rem(i, 2) == 0)
        def _():
            l_copy(l, lax.div(i, 2)).wait_send()

        x_copy(l, i).wait_send()

        @pl.when(z < last_z)
        def _():
            s_copy(l, i).wait_send()

        return carry

    lax.fori_loop(0, LAYERS * HC, sent, 0)
    for l in range(LAYERS):
        for d in range(1, n_tp):
            p_copy(l, d).wait_send()

    def moved(i, carry):
        o_copy(i).wait_send()
        o_copy(i).wait_recv()
        return carry

    lax.fori_loop(ROUND, RC, moved, 0)
    stream_copy().wait_send()
    scale_copy().wait_send()
    for hop in range(n_sec - 1):
        gated_round(hop).wait_send()
    for i in range(HALF):
        own_out(i).wait()
        if i:
            gated_copy(i).wait_send()
    for n in range(ROUND):
        for hop in range(n_sec - 1):
            round_copy(n, hop).wait_send()
        round_copy(n, n_sec - 2).wait_recv()


def hand_over(made, out, rows, sem):
    def part(n, way):
        at = pl.ds(32 * n, 32)
        if way == 0:
            return pltpu.make_async_copy(made.at[0, at], rows.at[at], sem.at[0, n])
        return pltpu.make_async_copy(rows.at[at], out.at[0, at], sem.at[1, n])

    for n in range(RC):
        part(n, 0).start()
    for n in range(RC):
        part(n, 0).wait()
        part(n, 1).start()
    for n in range(RC):
        part(n, 1).wait()


def per_device(sizes, *args):
    hbm = pl.BlockSpec(memory_space=pltpu.HBM)
    dma = pltpu.SemaphoreType.DMA
    n_sec, _, n_tp = sizes
    made = pl.pallas_call(
        functools.partial(kernel, *sizes),
        out_shape=jax.ShapeDtypeStruct((1, TOK, CH), BF16),
        in_specs=[hbm] * len(args),
        out_specs=hbm,
        scratch_shapes=[
            pltpu.VMEM((1, LAYERS, 32, TOK), F32),
            pltpu.VMEM((1, LAYERS, 32, TOK), F32),
            pltpu.VMEM((1, TOK), jnp.int32),
            pltpu.VMEM((1, LAYERS, 4, CH), F32),
            pltpu.VMEM((1, LAYERS, 4, 2, 128), F32),
            pltpu.SMEM((1, LAYERS, 32), F32),
            pltpu.VMEM((1, LAYERS, CH), F32),
            pltpu.VMEM((LAYERS + 1, BLK + TOK, CH), BF16),
            pltpu.VMEM((LAYERS, BLK + TOK, 256), BF16),
            pltpu.VMEM((1, TOK), jnp.int32),
            pltpu.VMEM((LAYERS, TOK, CH), BF16),
            pltpu.VMEM((3, TOK, 128), F32),
            pltpu.VMEM((128, CH), BF16),
            pltpu.VMEM((128, CH), BF16),
            pltpu.VMEM((LAYERS, NT, TOK, 128), F32),
            pltpu.VMEM((LAYERS, 32, TOK), F32),
            pltpu.VMEM((LAYERS, TOK, 128), BF16),
            pltpu.VMEM((LAYERS, TOK, 128), BF16),
            pltpu.VMEM((LAYERS, NT, 8, TOK), F32),
            pltpu.VMEM((LAYERS, TOK, 128), BF16),
            pltpu.VMEM((LAYERS, 128, TOK), BF16),
            pltpu.VMEM((LAYERS, 2, BLK, BLK), F32),
            pltpu.VMEM((TOK, CH), BF16),
            pltpu.VMEM((TOK, CH), BF16),
            pltpu.VMEM((NT, 128, TILE), BF16),
            pltpu.VMEM((LAYERS, NT, 144, TILE), BF16),
            pltpu.VMEM((LAYERS, HALF, 144, TILE), BF16),
            pltpu.VMEM((LAYERS, HC, 128, 128), BF16),
            pltpu.VMEM((LAYERS, HC, 128, 128), BF16),
            pltpu.VMEM((LAYERS, NT, 128, TILE), BF16),
            pltpu.VMEM((LAYERS, HC, 128, 128), BF16),
            pltpu.VMEM((TOK, CH), F32),
            pltpu.VMEM((TOK, CH), F32),
            pltpu.VMEM((TOK, 128), F32),
            pltpu.VMEM((LAYERS, 8, TOK), F32),
            pltpu.VMEM((LAYERS, max(n_tp - 1, 1), 8, TOK), F32),
            pltpu.VMEM((TOK, 128), F32),
            dma((14,)),
            dma((2, LAYERS)),
            dma((2, 2)),
            dma((2, LAYERS, HALF)),
            dma((2, LAYERS, HC)),
            dma((2, LAYERS, HC)),
            dma((2, LAYERS, max(n_tp - 1, 1))),
            dma((2, RC)),
            dma((2, n_sec - 1, ROUND)),
            pltpu.VMEM((max(n_sec - 2, 1), ROUND, 32, PART), BF16),
            dma((2, 2 + HALF)),
            dma((HALF,)),
            pltpu.VMEM((TOK, PART), BF16),
            pltpu.VMEM((8, TOK), F32),
            pltpu.VMEM((8, TOK), F32),
            pltpu.VMEM((HALF, TOK, TILE), BF16),
            pltpu.VMEM((HALF, TOK, TILE), BF16),
            dma((2, n_sec - 1)),
            pltpu.VMEM((max(n_sec - 2, 1), TOK, TILE), BF16),
        ],
        compiler_params=pltpu.CompilerParams(
            collective_id=0, has_side_effects=True, vmem_limit_bytes=60 * 1024 * 1024
        ),
        cost_estimate=pl.CostEstimate(
            flops=2_000_000_000, bytes_accessed=6_000_000, transcendentals=6_000_000
        ),
        name="mixer",
    )(*args)
    return pl.pallas_call(
        hand_over,
        out_shape=jax.ShapeDtypeStruct((1, TOK, CH), BF16),
        in_specs=[pl.BlockSpec(memory_space=pl.ANY)],
        out_specs=pl.BlockSpec(memory_space=pl.ANY),
        scratch_shapes=[pltpu.VMEM((TOK, CH), BF16), dma((2, RC))],
        name="hand_over",
        compiler_params=pltpu.CompilerParams(vmem_limit_bytes=60 * 1024 * 1024),
    )(made)


def solution(mesh):
    in_specs = (
        P("section", "ctx", "tp"),
        P("section", None, "ctx", "tp"),
        P("section", None, None, "ctx", "tp"),
        P("section", None, "tp", "ctx"),
        P("section", None, "tp", "ctx"),
        P("section", "ctx"),
        P("section", None, None, "tp"),
        P("section", None, None, None, "tp"),
        P("section", None, "tp"),
        P("section", None, "tp"),
    )
    out_specs = P("section", "ctx", "tp")
    sizes = tuple(mesh.shape[a] for a in ("section", "ctx", "tp"))
    return jax.shard_map(
        functools.partial(per_device, sizes),
        mesh=mesh,
        in_specs=in_specs,
        out_specs=out_specs,
        check_vma=False,
    )
```
